256 devices in a mesh: series: 16 (over z, core), tm: 16 (over y, x).
Axes of the slice: x: 4, y: 4, z: 8, core: 2. Of those that a mesh axis runs over, the one named last changes fastest.
Arguments:
- traffic: bfloat16 [32768, 32768], P('series', 'tm'), may hold values from -170 to 170
- sketch: float32 [32768, 64], P('tm'), may hold values from -0.03125 to 0.03125
Outputs:
- first: float32 [32768, 64], P('series')
- back_out: float32 [32768, 64], P('tm')
- basis: float32 [32768, 64], P('series')
- projection: float32 [64, 32768], P(None, 'tm')
The draws below stay inside these ranges and needn't reach their ends.
All inputs are finite; a program needn't handle non-finite values.
Results may differ from the reference program's by a relative error of at most 0.0003.
Values sent between devices are 32-bit elements; how exact they have to be, the bound alone decides.
A program may use at most 64 MiB of HBM per device.

```python
import jax
import jax.numpy as jnp
from jax import lax

R_DEV = 2048
K = 64
M = 32768
N = 32768
N_SERIES = 16


def draw_traffic(key, part):
    key = jax.random.fold_in(key, 7)
    values = jnp.clip(jax.random.normal(key, (M, N), jnp.float32), -6.0, 6.0)
    spread = 1.386
    row_pos = jnp.arange(M, dtype=jnp.float32) / jnp.float32(M - 1)
    col_pos = jnp.arange(N, dtype=jnp.float32) / jnp.float32(N - 1)
    row_scale = jnp.exp(spread * row_pos)
    col_scale = jnp.exp(spread * col_pos)
    return (values * row_scale[:, None] * col_scale[None, :]).astype(jnp.bfloat16)


def block_levels(stream_key, shape, shards, low, high):
    gain, own = 1.0, jax.random.fold_in(stream_key, 6)
    for dim, blocks in shards:
        draws = jnp.exp(jax.random.uniform(jax.random.fold_in(own, dim), (blocks,), jnp.float32, low / len(shards), high / len(shards)))
        gain = gain * jnp.repeat(draws, shape[dim] // blocks).reshape([-1 if axis == dim else 1 for axis in range(len(shape))])
    return gain


def bell_draw(stream_key, extent, scale, reach, cuts=(), kind=jnp.bfloat16):
    array = scale * jax.random.normal(stream_key, extent, jnp.float32)
    if cuts:
        array = array * block_levels(stream_key, extent, cuts, -0.22, 0.18)
    return jnp.clip(array, -reach, reach).astype(kind)


def setup_inputs(seed: int = 0) -> dict:
    seeds = jax.random.split(jax.random.key(seed), 3)
    traffic = draw_traffic(jax.random.fold_in(seeds[2], 71), 0)
    sketch = bell_draw(seeds[1], (N, K), N ** -0.5, 0.03125, ((0, 16),), jnp.float32)
    return {"traffic": traffic, "sketch": sketch}


def orthonormal(tall):
    gram = jnp.dot(tall.T.astype(jnp.float32), tall.astype(jnp.float32), precision=lax.Precision.HIGHEST, preferred_element_type=jnp.float32)
    lower = jnp.linalg.cholesky(gram)
    return jax.scipy.linalg.solve_triangular(lower, tall.T, lower=True).T

def times_right(traffic, panel):
    blocks = traffic.reshape(N_SERIES, R_DEV, N)

    def one_block(block):
        return jnp.dot(block.astype(jnp.float32), panel.astype(jnp.float32), precision=lax.Precision.HIGHEST, preferred_element_type=jnp.float32)
    return lax.map(one_block, blocks).reshape(M, panel.shape[1])

def times_left(traffic, panel):
    blocks = traffic.reshape(N_SERIES, R_DEV, N)
    rows = panel.reshape(N_SERIES, R_DEV, panel.shape[1])

    def add_block(total, pair):
        block, part = pair
        term = lax.dot_general(part.astype(jnp.float32), block.astype(jnp.float32), (((0,), (0,)), ((), ())), precision=lax.Precision.HIGHEST, preferred_element_type=jnp.float32)
        return (total + term, None)
    start = jnp.zeros((panel.shape[1], N), jnp.float32)
    total, unused = lax.scan(add_block, start, (blocks, rows))
    return total

def reference(traffic, sketch):
    sampled = times_right(traffic, sketch)
    first_basis = orthonormal(sampled)
    first = jnp.sqrt(jnp.float32(M)) * first_basis
    back = times_left(traffic, first_basis).T
    back_basis = orthonormal(back)
    back_out = jnp.sqrt(jnp.float32(N)) * back_basis
    forward = times_right(traffic, back_basis)
    final_basis = orthonormal(forward)
    basis = jnp.sqrt(jnp.float32(M)) * final_basis
    projection = times_left(traffic, final_basis)
    return (first, back_out, basis, projection)
```

```python
import functools

import jax
import jax.numpy as jnp
from jax import lax
from jax.experimental import pallas as pl
from jax.experimental.pallas import tpu as pltpu
from jax.sharding import PartitionSpec as P

F32, BF16 = jnp.float32, jnp.bfloat16
HIGHEST = lax.Precision.HIGHEST
MESH = pl.DeviceIdType.MESH
LANES = 128
PAIR = 2 * LANES
NN = (((1,), (0,)), ((), ()))
NT = (((1,), (1,)), ((), ()))
CUTS = (24, 48)


def far_first(k, n):
    half = n // 2
    return (k + half + k // half + half * (k // (n - 1))) % n


def exact(x, y, dims=NN):
    return lax.dot_general(x, y, dims, precision=HIGHEST, preferred_element_type=F32)


def kernel(
    n_s, n_t, a_hbm, sketch, first_out, back_out, basis_out, proj_out,
    a, lhs, tm_part, tm_in, tm_full, z_part, sib_in, z_send, z_in, z_full, flats, back_flat, basis_flat, invs, work,
    g_out, g_tm, g_z, g_half, g_sib,
    a_sem, tm_rs_s, tm_rs_r, tm_ag_s, tm_ag_r, sib_s, sib_r, z_rs_s, z_rs_r, z_ag_s, z_ag_r, fw_s, fw_r,
    g_s, g_r, gs_s, gs_r,
):
    n_z, n_p = n_s // 2, n_t // 2
    k_all = sketch.shape[0]
    k_half = k_all // 2
    rows, cols = a.shape
    rows_total, cols_total = rows * n_s, cols * n_t
    s, t = lax.axis_index("series"), lax.axis_index("tm")
    z, core, p_me = s // 2, s % 2, t // 2
    halves = (pl.ds(0, k_half), pl.ds(k_half, k_half))

    def remote(src, dst, send, recv, to_s, to_t):
        return pltpu.make_async_remote_copy(
            src_ref=src, dst_ref=dst, send_sem=send, recv_sem=recv, device_id=(to_s, to_t), device_id_type=MESH
        )

    def to_sibling(src, dst, send, recv):
        return remote(src, dst, send, recv, 2 * z + 1 - core, t)

    def settle(ref, sem):
        pltpu.make_async_copy(ref, ref, sem).wait()

    def loop(n, body):
        def step(k, carry):
            body(k)
            return carry

        lax.fori_loop(0, n, step, 0)

    barrier = pltpu.get_barrier_semaphore()

    def greet_tm(k):
        pl.semaphore_signal(barrier, inc=1, device_id=(s, (t + 1 + k) % n_t), device_id_type=MESH)

    def greet_z(k):
        pl.semaphore_signal(barrier, inc=1, device_id=(2 * ((z + 1 + k) % n_z) + core, t), device_id_type=MESH)

    loop(n_t - 1, greet_tm)
    loop(n_z - 1, greet_z)
    pl.semaphore_signal(barrier, inc=1, device_id=(2 * z + 1 - core, t), device_id_type=MESH)

    def a_copy(k):
        p = (p_me + far_first(k, n_p)) % n_p
        block = pl.ds(pl.multiple_of(p * PAIR, PAIR), PAIR)
        return pltpu.make_async_copy(a_hbm.at[block, :], a.at[block, :], a_sem.at[k])

    loop(n_p, lambda k: a_copy(k).start())

    def split(x, h, lanes):
        for term in range(3):
            low = x.astype(BF16)
            lhs[pl.ds((3 * h + term) * k_half, k_half), lanes] = low
            x = x - low.astype(F32)

    def join(acc, h):
        b = 3 * h * k_half
        return acc[b : b + k_half] + (acc[b + k_half : b + 2 * k_half] + acc[b + 2 * k_half : b + 3 * k_half])

    for h in range(2):
        split(sketch[halves[h], :], h, slice(None))

    def tm_product(stage, ready):
        part, into = tm_part.at[stage], tm_in.at[stage]

        def send(k, h):
            p = (p_me + far_first(k, n_p)) % n_p
            for e in range(2):
                to = 2 * p + e

                @pl.when(to != t)
                def _():
                    remote(
                        part.at[to, halves[h], :], into.at[(t - to - 1 + n_t) % n_t, halves[h], :],
                        tm_rs_s.at[stage, h], tm_rs_r.at[stage, h], s, to,
                    ).start()

        def body(k):
            if ready is not None:
                ready(k)
            p = (p_me + far_first(k, n_p)) % n_p
            block = a[pl.ds(pl.multiple_of(p * PAIR, PAIR), PAIR), :]
            acc = lax.dot_general(lhs[...], block, NT, preferred_element_type=F32)
            for h in range(2):
                val = join(acc, h)
                for e in range(2):
                    part[2 * p + e, halves[h], :] = val[:, e * LANES : (e + 1) * LANES]
            send(k, 0)

        loop(n_p, body)
        loop(n_p, lambda k: send(k, 1))

    def tm_sum(stage, h):
        settle(tm_in.at[stage, :, halves[h], :], tm_rs_r.at[stage, h])
        total = tm_part[stage, t, halves[h], :]
        for i in range(n_t - 1):
            total = total + tm_in[stage, i, halves[h], :]
        return total

    def tm_gather(stage, h, chunk):
        tm_full[stage, t, halves[h], :] = chunk

        def send(k):
            mine = tm_full.at[stage, t, halves[h], :]
            to = (t + 1 + (k + n_t // 2 - 1) % (n_t - 1)) % n_t
            remote(mine, mine, tm_ag_s.at[stage, h], tm_ag_r.at[stage, h], s, to).start()

        loop(n_t - 1, send)

    def tm_take(stage, h, flat):
        settle(tm_full.at[stage, pl.ds(0, n_t - 1), halves[h], :], tm_ag_r.at[stage, h])
        for c in range(n_t):
            lanes = pl.ds(c * LANES, LANES)
            x = tm_full[stage, c, halves[h], :]
            flat[halves[h], lanes] = x
            split(x, h, lanes)

    def z_product(stage):
        part = z_part.at[stage]

        def pair(k):
            return (z + far_first(k, n_z)) % n_z

        def sibling(p):
            return to_sibling(part.at[1 - core, p], sib_in.at[stage, p], sib_s.at[stage, p], sib_r.at[stage, p])

        def send(k, h):
            p = pair(k)
            remote(
                z_send.at[stage, p, halves[h], :], z_in.at[stage, (z - p - 1 + n_z) % n_z, halves[h], :],
                z_rs_s.at[stage, h], z_rs_r.at[stage, h], 2 * p + core, t,
            ).start()

        def both(k):
            p = pair(k)
            sibling(p).wait_recv()
            z_send[stage, p] = part[core, p] + sib_in[stage, p]

        def body(k):
            p = pair(k)
            block = a[:, pl.ds(pl.multiple_of(p * PAIR, PAIR), PAIR)]
            acc = lax.dot_general(lhs[...], block, NN, preferred_element_type=F32)
            for h in range(2):
                val = join(acc, h)
                for e in range(2):
                    part[e, p, halves[h], :] = val[:, e * LANES : (e + 1) * LANES]
            sibling(p).start()

            @pl.when(k > 0)
            def _():
                both(k - 1)
                send(k - 1, 0)

        loop(n_z, body)
        loop(n_z - 1, lambda k: send(k, 1))
        both(n_z - 1)

    def z_sum(stage, h):
        settle(z_in.at[stage, :, halves[h], :], z_rs_r.at[stage, h])
        total = z_send[stage, z, halves[h], :]
        for i in range(n_z - 1):
            total = total + z_in[stage, i, halves[h], :]
        return total

    def z_gather(stage, h, chunk):
        z_full[stage, core, z, halves[h], :] = chunk

        def send(k):
            mine = z_full.at[stage, core, z, halves[h], :]
            to = (z + far_first(k, n_z)) % n_z
            remote(mine, mine, z_ag_s.at[stage, h], z_ag_r.at[stage, h], 2 * to + core, t).start()

        loop(n_z - 1, send)

    def z_forward(stage, h):
        settle(z_full.at[stage, core, pl.ds(0, n_z - 1), halves[h], :], z_ag_r.at[stage, h])
        mine = z_full.at[stage, core, :, halves[h], :]
        to_sibling(mine, mine, fw_s.at[stage, h], fw_r.at[stage, h]).start()

    def z_take(stage, h, flat, again=True):
        settle(z_full.at[stage, core, :, halves[h], :], fw_r.at[stage, h])
        for c in range(n_s):
            lanes = pl.ds(c * LANES, LANES)
            x = z_full[stage, c % 2, c // 2, halves[h], :]
            flat[halves[h], lanes] = x
            if again:
                split(x, h, lanes)

    def pack(flat, out):
        gram = exact(flat[...], flat[...], NT)
        out[:, :k_all] = gram[:k_half]
        out[:, k_all:] = gram[k_half:]

    def unpack(packed):
        lane = lax.broadcasted_iota(jnp.int32, (k_all, 2 * k_all), 1)
        row = lax.broadcasted_iota(jnp.int32, (k_all, 2 * k_all), 0)
        work[...] = jnp.where(lane == row + k_all, 1.0, 0.0).astype(F32)
        work[:k_half, :k_all] = packed[:, :k_all]
        work[k_half:, :k_all] = packed[:, k_all:]

    def gram_z_send(i, flat):
        pack(flat, g_out.at[i])
        slot = g_z.at[i // 2, z]
        slot[...] = g_out[i]

        def send(k):
            to = (z + far_first(k, n_z)) % n_z
            remote(g_out.at[i], slot, g_s.at[i], g_r.at[i], 2 * to + core, t).start()

        loop(n_z - 1, send)

    def gram_z_middle(i):
        b = i // 2
        settle(g_z.at[b, pl.ds(0, n_z - 1)], g_r.at[i])
        total = g_z[b, 0]
        for k in range(1, n_z):
            total = total + g_z[b, k]
        g_half[b] = total
        to_sibling(g_half.at[b], g_sib.at[b], gs_s.at[b], gs_r.at[b]).start()

    def gram_z_end(i):
        b = i // 2
        settle(g_sib.at[b], gs_r.at[b])
        unpack(g_half[b] + g_sib[b])

    def gram_tm_send(i, flat):
        pack(flat, g_out.at[i])
        slot = g_tm.at[t]
        slot[...] = g_out[i]

        def send(k):
            to = (t + 1 + (k + n_t // 2 - 1) % (n_t - 1)) % n_t
            remote(g_out.at[i], slot, g_s.at[i], g_r.at[i], s, to).start()

        loop(n_t - 1, send)

    def gram_tm_end(i):
        settle(g_tm.at[pl.ds(0, n_t - 1)], g_r.at[i])
        total = g_tm[0]
        for k in range(1, n_t):
            total = total + g_tm[k]
        unpack(total)

    def eliminate(start, stop):
        x = work[...]
        row = lax.broadcasted_iota(jnp.int32, (k_all, 1), 0)
        for j in range(start, stop):
            factor = jnp.where(row > j, x[:, j : j + 1] * (1.0 / x[j : j + 1, j : j + 1]), 0.0)
            x = x - factor * x[j : j + 1, :]
        work[...] = x

    def inverse(i):
        x = work[...]
        lane = lax.broadcasted_iota(jnp.int32, (k_all, 2 * k_all), 1)
        row = lax.broadcasted_iota(jnp.int32, (k_all, 2 * k_all), 0)
        diag = jnp.sum(jnp.where(lane == row, x, 0.0), axis=1, keepdims=True)
        invs[i] = (x * lax.rsqrt(diag))[:, k_all:]

    def apply_a(i, low):
        return exact(invs[i, :k_half, :k_half], low)

    def apply_b(i, low, high):
        return exact(invs[i, k_half:, :k_half], low) + exact(invs[i, k_half:, k_half:], high)

    cut_1, cut_2 = CUTS

    def ready(k):
        a_copy(k).wait()

        @pl.when(k == 0)
        def _():
            pl.semaphore_wait(barrier, n_t - 1 + n_z - 1 + 1)

    tm_product(0, ready)
    for h in range(2):
        tm_gather(0, h, tm_sum(0, h))
    for h in range(2):
        tm_take(0, h, flats.at[0])

    gram_z_send(0, flats.at[0])
    z_product(0)
    z_gather(0, 0, z_sum(0, 0))
    gram_z_middle(0)
    z_gather(0, 1, z_sum(0, 1))
    gram_z_end(0)
    eliminate(0, cut_1)
    z_forward(0, 0)
    eliminate(cut_1, cut_2)
    z_forward(0, 1)
    eliminate(cut_2, k_all)
    inverse(0)
    for h in range(2):
        z_take(0, h, flats.at[1])

    back_flat[...] = exact(invs[0], flats[1])
    gram_tm_send(1, back_flat)
    tm_product(1, None)
    first_out[...] = (rows_total**0.5) * exact(invs[0], flats[0])
    low = tm_sum(1, 0)
    tm_gather(1, 0, apply_a(0, low))
    high = tm_sum(1, 1)
    tm_gather(1, 1, apply_b(0, low, high))
    gram_tm_end(1)
    eliminate(0, cut_1)
    tm_take(1, 0, flats.at[2])
    eliminate(cut_1, k_all)
    inverse(1)
    tm_take(1, 1, flats.at[2])

    basis_flat[...] = exact(invs[1], flats[2])
    gram_z_send(2, basis_flat)
    z_product(1)
    back_out[...] = (cols_total**0.5) * exact(invs[1], back_flat[...])
    low = z_sum(1, 0)
    z_gather(1, 0, apply_a(1, low))
    gram_z_middle(2)
    high = z_sum(1, 1)
    z_gather(1, 1, apply_b(1, low, high))
    gram_z_end(2)
    eliminate(0, cut_1)
    z_forward(1, 0)
    eliminate(cut_1, cut_2)
    z_forward(1, 1)
    eliminate(cut_2, k_all)
    inverse(2)
    basis_out[...] = (rows_total**0.5) * exact(invs[2], basis_flat[...])
    for h in range(2):
        z_take(1, h, flats.at[3], again=False)
    proj_out[...] = exact(invs[2], flats[3])

    for stage in range(2):
        for h in range(2):
            settle(tm_in.at[stage, :, halves[h], :], tm_rs_s.at[stage, h])
            settle(tm_full.at[stage, pl.ds(0, n_t - 1), halves[h], :], tm_ag_s.at[stage, h])
            settle(z_in.at[stage, :, halves[h], :], z_rs_s.at[stage, h])
            settle(z_full.at[stage, core, pl.ds(0, n_z - 1), halves[h], :], z_ag_s.at[stage, h])
            settle(z_full.at[stage, core, :, halves[h], :], fw_s.at[stage, h])
        for p in range(n_z):
            settle(sib_in.at[stage, p], sib_s.at[stage, p])
        settle(g_z.at[stage, pl.ds(0, n_z - 1)], g_s.at[2 * stage])
        settle(g_sib.at[stage], gs_s.at[stage])
    settle(g_tm.at[pl.ds(0, n_t - 1)], g_s.at[1])


def solution(mesh):
    n_s, n_t = mesh.shape["series"], mesh.shape["tm"]
    n_z = n_s // 2

    def local(traffic, sketch):
        rows, cols = traffic.shape
        k = sketch.shape[1]
        vmem = pl.BlockSpec(memory_space=pltpu.VMEM)
        sem = pltpu.SemaphoreType.DMA
        chunk = (k, LANES)
        gram = (k // 2, 2 * k)
        outs = pl.pallas_call(
            functools.partial(kernel, n_s, n_t),
            out_shape=(
                jax.ShapeDtypeStruct((k, rows), F32),
                jax.ShapeDtypeStruct((k, cols), F32),
                jax.ShapeDtypeStruct((k, rows), F32),
                jax.ShapeDtypeStruct((k, cols), F32),
            ),
            in_specs=[pl.BlockSpec(memory_space=pl.ANY), vmem],
            out_specs=(vmem,) * 4,
            scratch_shapes=[
                pltpu.VMEM((rows, cols), BF16),
                pltpu.VMEM((3 * k, cols), BF16),
                pltpu.VMEM((2, n_t, *chunk), F32),
                pltpu.VMEM((2, n_t - 1, *chunk), F32),
                pltpu.VMEM((2, n_t, *chunk), F32),
                pltpu.VMEM((2, 2, n_z, *chunk), F32),
                pltpu.VMEM((2, n_z, *chunk), F32),
                pltpu.VMEM((2, n_z, *chunk), F32),
                pltpu.VMEM((2, n_z - 1, *chunk), F32),
                pltpu.VMEM((2, 2, n_z, *chunk), F32),
                pltpu.VMEM((4, k, cols), F32),
                pltpu.VMEM((k, cols), F32),
                pltpu.VMEM((k, rows), F32),
                pltpu.VMEM((3, k, k), F32),
                pltpu.VMEM((k, 2 * k), F32),
                pltpu.VMEM((3, *gram), F32),
                pltpu.VMEM((n_t, *gram), F32),
                pltpu.VMEM((2, n_z, *gram), F32),
                pltpu.VMEM((2, *gram), F32),
                pltpu.VMEM((2, *gram), F32),
                sem((n_t // 2,)),
                sem((2, 2)), sem((2, 2)), sem((2, 2)), sem((2, 2)),
                sem((2, n_z)), sem((2, n_z)),
                sem((2, 2)), sem((2, 2)), sem((2, 2)), sem((2, 2)), sem((2, 2)), sem((2, 2)),
                sem((3,)), sem((3,)), sem((2,)), sem((2,)),
            ],
            compiler_params=pltpu.CompilerParams(
                collective_id=0, has_side_effects=True, vmem_limit_bytes=48 * 2**20
            ),
            name="range_finder",
        )(traffic, sketch.T)
        return outs[0].T, outs[1].T, outs[2].T, outs[3]

    in_specs = (P("series", "tm"), P("tm", None))
    out_specs = (P("series", None), P("tm", None), P("series", None), P(None, "tm"))
    return jax.shard_map(local, mesh=mesh, in_specs=in_specs, out_specs=out_specs, check_vma=False)
```

```python
import functools
import math

import jax
import jax.numpy as jnp
from jax import lax
from jax.experimental import pallas as pl
from jax.experimental.pallas import tpu as pltpu
from jax.sharding import PartitionSpec as P

F32, BF16 = jnp.float32, jnp.bfloat16
HIGHEST = lax.Precision.HIGHEST
MESH = pl.DeviceIdType.MESH
LANES = 128
PANEL = 8
NN = (((1,), (0,)), ((), ()))
NT = (((1,), (1,)), ((), ()))


def far_first(n):
    return sorted(range(n), key=lambda d: (-min(d, n - d), d))


def exact(x, y, dims=NN):
    return lax.dot_general(x, y, dims, precision=HIGHEST, preferred_element_type=F32)


def kernel(
    n_s, n_t, a_hbm, sketch_hbm, first_out, back_out, basis_out, proj_out, inv_out,
    a, sketch, lhs, tm_part, tm_in, tm_full, z_part, sib_in, z_send, z_in, z_full, flats, back_flat, basis_flat, tm_low, z_low, invs, work,
    g_out, g_tm, g_z, g_half, g_sib,
    a_sem, s_sem, tm_rs_s, tm_rs_r, tm_ag_s, tm_ag_r, sib_s, sib_r, z_rs_s, z_rs_r, z_ag_s, z_ag_r, fw_s, fw_r,
    g_s, g_r, gs_s, gs_r,
):
    n_z, n_g = n_s // 2, n_s // 4
    n_x = math.isqrt(n_t)
    n_y = n_t // n_x
    k_all = sketch.shape[0]
    k_half = k_all // 2
    rows, cols = a.shape
    rows_total, cols_total = rows * n_s, cols * n_t
    s, t = lax.axis_index("series"), lax.axis_index("tm")
    z, core, y, x = s // 2, s % 2, t // n_x, t % n_x
    other = 2 * z + 1 - core
    halves = (pl.ds(0, k_half), pl.ds(k_half, k_half))

    tm_y = {d: (y + d) % n_y for d in range(n_y)}
    tm_x = {d: (x + d) % n_x for d in range(n_x)}
    tm_to = {(dy, dx): tm_y[dy] * n_x + tm_x[dx] for dy in range(n_y) for dx in range(n_x)}
    z_to = {d: (z + d) % n_z for d in range(n_z)}
    z_group = {d: (z // 2 + d) % n_g for d in range(n_g)}
    tm_order = sorted((o for o in tm_to if o != (0, 0)), key=lambda o: -min(o[0], n_y - o[0]) - min(o[1], n_x - o[1]))
    z_order = [d for d in far_first(n_z) if d]

    def remote(src, dst, send, recv, to_s, to_t):
        return pltpu.make_async_remote_copy(
            src_ref=src, dst_ref=dst, send_sem=send, recv_sem=recv, device_id=(to_s, to_t), device_id_type=MESH
        )

    def settle(ref, sem):
        pltpu.make_async_copy(ref, ref, sem).wait()

    barrier = pltpu.get_barrier_semaphore()
    greeted = [(s, tm_to[o]) for o in tm_order] + [(2 * z_to[d] + core, t) for d in z_order] + [(other, t)]
    for device in greeted:
        pl.semaphore_signal(barrier, inc=1, device_id=device, device_id_type=MESH)

    block_rows = n_x * LANES

    def tm_block(dy):
        return pl.ds(pl.multiple_of(tm_y[dy] * block_rows, block_rows), block_rows)

    sketch_copy = pltpu.make_async_copy(sketch_hbm, sketch, s_sem)
    sketch_copy.start()
    a_copies = {dy: pltpu.make_async_copy(a_hbm.at[tm_block(dy), :], a.at[tm_block(dy), :], a_sem.at[dy]) for dy in range(n_y)}
    for dy in far_first(n_y):
        a_copies[dy].start()

    def split(v, h, lanes):
        for term in range(3):
            low = v.astype(BF16)
            lhs[pl.ds((3 * h + term) * k_half, k_half), lanes] = low
            v = v - low.astype(F32)

    def terms(h):
        return lhs[pl.ds(3 * h * k_half, 3 * k_half), :]

    def join(acc):
        return acc[:k_half] + (acc[k_half : 2 * k_half] + acc[2 * k_half :])

    def tm_product(stage, h, between=None, ready=None):
        for i, dy in enumerate(far_first(n_y)):
            if ready is not None:
                ready(dy)
            acc = lax.dot_general(terms(h), a[tm_block(dy), :], NT, preferred_element_type=F32)
            val = join(acc)
            for e in range(n_x):
                tm_part[stage, tm_y[dy] * n_x + e, halves[h], :] = val[:, e * LANES : (e + 1) * LANES]
            for dx in far_first(n_x):
                if (dy, dx) != (0, 0):
                    to = tm_to[dy, dx]
                    remote(
                        tm_part.at[stage, to, halves[h], :], tm_in.at[stage, t, halves[h], :],
                        tm_rs_s.at[stage, h], tm_rs_r.at[stage, h], s, to,
                    ).start()
            if between and i == min(between[0], n_y - 1):
                between[1]()

    def tm_sum(stage, h):
        settle(tm_in.at[stage, pl.ds(0, n_t - 1), halves[h], :], tm_rs_r.at[stage, h])
        tm_in[stage, t, halves[h], :] = tm_part[stage, t, halves[h], :]
        total = tm_in[stage, 0, halves[h], :]
        for i in range(1, n_t):
            total = total + tm_in[stage, i, halves[h], :]
        return total

    def tm_gather(stage, h, chunk):
        tm_full[stage, t, halves[h], :] = chunk
        mine = tm_full.at[stage, t, halves[h], :]
        for o in tm_order:
            remote(mine, mine, tm_ag_s.at[stage, h], tm_ag_r.at[stage, h], s, tm_to[o]).start()

    def tm_take(stage, h, flat):
        settle(tm_full.at[stage, pl.ds(0, n_t - 1), halves[h], :], tm_ag_r.at[stage, h])
        for c in range(n_t):
            lanes = pl.ds(c * LANES, LANES)
            v = tm_full[stage, c, halves[h], :]
            flat[halves[h], lanes] = v
            split(v, h, lanes)

    def z_pair(dg):
        return pl.ds(2 * z_group[dg], 2)

    def sibling(stage, h, dg):
        return remote(
            z_part.at[stage, 1 - core, z_pair(dg), halves[h], :], sib_in.at[stage, z_pair(dg), halves[h], :],
            sib_s.at[stage, h, dg], sib_r.at[stage, h, dg], other, t,
        )

    def z_both(stage, h, dg):
        sibling(stage, h, dg).wait_recv()
        pair = z_pair(dg)
        z_send[stage, pair, halves[h], :] = z_part[stage, core, pair, halves[h], :] + sib_in[stage, pair, halves[h], :]
        tos = [2 * z_group[dg] + e for e in range(2)] if dg else [4 * (z // 2) + 1 - z]
        for to in tos:
            remote(
                z_send.at[stage, to, halves[h], :], z_in.at[stage, z, halves[h], :],
                z_rs_s.at[stage, h], z_rs_r.at[stage, h], 2 * to + core, t,
            ).start()

    def z_product(stage, h, between=None):
        before = None
        for i, dg in enumerate(far_first(n_g)):
            block = pl.ds(pl.multiple_of(z_group[dg] * 4 * LANES, 4 * LANES), 4 * LANES)
            acc = lax.dot_general(terms(h), a[:, block], NN, preferred_element_type=F32)
            val = join(acc)
            for e in range(4):
                z_part[stage, e % 2, 2 * z_group[dg] + e // 2, halves[h], :] = val[:, e * LANES : (e + 1) * LANES]
            sibling(stage, h, dg).start()
            if before is not None:
                z_both(stage, h, before)
            before = dg
            if between and i == min(between[0], n_g - 1):
                between[1]()

    def z_sum(stage, h):
        settle(z_in.at[stage, pl.ds(0, n_z - 1), halves[h], :], z_rs_r.at[stage, h])
        z_in[stage, z, halves[h], :] = z_send[stage, z, halves[h], :]
        total = z_in[stage, 0, halves[h], :]
        for i in range(1, n_z):
            total = total + z_in[stage, i, halves[h], :]
        return total

    def z_gather(stage, h, chunk):
        z_full[stage, core, z, halves[h], :] = chunk
        mine = z_full.at[stage, core, z, halves[h], :]
        for d in z_order:
            remote(mine, mine, z_ag_s.at[stage, h], z_ag_r.at[stage, h], 2 * z_to[d] + core, t).start()

    def z_forward(stage, h):
        settle(z_full.at[stage, core, pl.ds(0, n_z - 1), halves[h], :], z_ag_r.at[stage, h])
        mine = z_full.at[stage, core, :, halves[h], :]
        remote(mine, mine, fw_s.at[stage, h], fw_r.at[stage, h], other, t).start()

    def z_take(stage, h, flat, again=True):
        settle(z_full.at[stage, core, :, halves[h], :], fw_r.at[stage, h])
        for c in range(n_s):
            lanes = pl.ds(c * LANES, LANES)
            v = z_full[stage, c % 2, c // 2, halves[h], :]
            flat[halves[h], lanes] = v
            if again:
                split(v, h, lanes)

    def pack(flat, out):
        gram = exact(flat[...], flat[...], NT)
        out[:, :k_all] = gram[:k_half]
        out[:, k_all:] = gram[k_half:]

    def gram_z_send(i, flat):
        pack(flat, g_out.at[i])
        slot = g_z.at[i // 2, z]
        slot[...] = g_out[i]
        for d in z_order:
            remote(g_out.at[i], slot, g_s.at[i], g_r.at[i], 2 * z_to[d] + core, t).start()

    def gram_z_middle(i):
        b = i // 2
        settle(g_z.at[b, pl.ds(0, n_z - 1)], g_r.at[i])
        total = g_z[b, 0]
        for k in range(1, n_z):
            total = total + g_z[b, k]
        g_half[b] = total
        remote(g_half.at[b], g_sib.at[b], gs_s.at[b], gs_r.at[b], other, t).start()

    def gram_z_end(i):
        b = i // 2
        settle(g_sib.at[b], gs_r.at[b])
        return g_half[b] + g_sib[b]

    def gram_tm_send(i, flat):
        pack(flat, g_out.at[i])
        slot = g_tm.at[t]
        slot[...] = g_out[i]
        for o in tm_order:
            remote(g_out.at[i], slot, g_s.at[i], g_r.at[i], s, tm_to[o]).start()

    def gram_tm_end(i):
        settle(g_tm.at[pl.ds(0, n_t - 1)], g_r.at[i])
        total = g_tm[0]
        for k in range(1, n_t):
            total = total + g_tm[k]
        return total

    def invert(i, packed):
        lane = lax.broadcasted_iota(jnp.int32, (k_all, 2 * k_all), 1)
        row = lax.broadcasted_iota(jnp.int32, (k_all, 2 * k_all), 0)
        work[...] = jnp.where(lane == row + k_all, 1.0, 0.0).astype(F32)
        work[:k_half, :k_all] = packed[:, :k_all]
        work[k_half:, :k_all] = packed[:, k_all:]
        v = work[...]
        for j in range(0, k_all, PANEL):
            col = [jnp.broadcast_to(v[:, j + m : j + m + 1], v.shape) for m in range(PANEL)]
            line = [v[j + m : j + m + 1, :] for m in range(PANEL)]
            for m in range(PANEL):
                factor = jnp.where(row > j + m, col[m] * (1.0 / col[m][j + m : j + m + 1, :]), 0.0)
                for n in range(m + 1, PANEL):
                    line[n] = line[n] - factor[j + n : j + n + 1, :] * line[m]
                    col[n] = col[n] - factor * col[n][j + m : j + m + 1, :]
                v = v - factor * line[m]
        diag = jnp.sum(jnp.where(lane == row, v, 0.0), axis=1, keepdims=True)
        invs[i] = (v * lax.rsqrt(diag))[:, k_all:]

    def apply_a(i, low):
        return exact(invs[i, :k_half, :k_half], low)

    def apply_b(i, low, high):
        return exact(invs[i, k_half:, :k_half], low) + exact(invs[i, k_half:, k_half:], high)

    sketch_copy.wait()
    for h in range(2):
        split(sketch[halves[h], :], h, slice(None))

    def ready(dy):
        a_copies[dy].wait()
        if dy == far_first(n_y)[0]:
            pl.semaphore_wait(barrier, len(greeted))

    tm_product(0, 0, ready=ready)
    tm_product(0, 1)
    tm_gather(0, 0, tm_sum(0, 0))
    tm_gather(0, 1, tm_sum(0, 1))
    tm_take(0, 0, flats.at[0])

    z_product(0, 0)
    tm_take(0, 1, flats.at[0])
    z_both(0, 0, 0)
    z_product(0, 1, (2, lambda: z_gather(0, 0, z_sum(0, 0))))
    gram_z_send(0, flats.at[0])
    z_both(0, 1, 0)
    z_gather(0, 1, z_sum(0, 1))
    z_forward(0, 0)
    gram_z_middle(0)
    z_take(0, 0, flats.at[1])

    tm_product(1, 0)
    z_forward(0, 1)
    invert(0, gram_z_end(0))
    z_take(0, 1, flats.at[1])

    def tm_first_half():
        tm_low[...] = tm_sum(1, 0)
        tm_gather(1, 0, apply_a(0, tm_low[...]))

    tm_product(1, 1, (0, tm_first_half))
    back_flat[...] = exact(invs[0], flats[1])
    gram_tm_send(1, back_flat)
    first_out[...] = (rows_total**0.5) * exact(invs[0], flats[0])
    tm_gather(1, 1, apply_b(0, tm_low[...], tm_sum(1, 1)))
    tm_take(1, 0, flats.at[2])

    z_product(1, 0)
    z_both(1, 0, 0)
    invert(1, gram_tm_end(1))
    tm_take(1, 1, flats.at[2])

    def z_first_half():
        z_low[...] = z_sum(1, 0)
        z_gather(1, 0, apply_a(1, z_low[...]))

    z_product(1, 1, (1, z_first_half))
    basis_flat[...] = exact(invs[1], flats[2])
    gram_z_send(2, basis_flat)
    z_both(1, 1, 0)
    back_out[...] = (cols_total**0.5) * exact(invs[1], back_flat[...])
    z_gather(1, 1, apply_b(1, z_low[...], z_sum(1, 1)))
    z_forward(1, 0)
    gram_z_middle(2)
    invert(2, gram_z_end(2))
    inv_out[...] = invs[2]
    z_forward(1, 1)
    basis_out[...] = (rows_total**0.5) * exact(invs[2], basis_flat[...])
    for h in range(2):
        z_take(1, h, proj_out, again=False)

    for stage in range(2):
        for h in range(2):
            settle(tm_in.at[stage, pl.ds(0, n_t - 1), halves[h], :], tm_rs_s.at[stage, h])
            settle(z_in.at[stage, pl.ds(0, n_z - 1), halves[h], :], z_rs_s.at[stage, h])
            settle(tm_full.at[stage, pl.ds(0, n_t - 1), halves[h], :], tm_ag_s.at[stage, h])
            settle(z_full.at[stage, core, pl.ds(0, n_z - 1), halves[h], :], z_ag_s.at[stage, h])
            settle(z_full.at[stage, core, :, halves[h], :], fw_s.at[stage, h])
            for dg in range(n_g):
                settle(sib_in.at[stage, pl.ds(0, 2), halves[h], :], sib_s.at[stage, h, dg])
        settle(g_z.at[stage, pl.ds(0, n_z - 1)], g_s.at[2 * stage])
        settle(g_sib.at[stage], gs_s.at[stage])
    settle(g_tm.at[pl.ds(0, n_t - 1)], g_s.at[1])


def finish(first_in, back_in, basis_in, proj_in, inv, first_out, back_out, basis_out, proj_out, sems):
    pairs = ((first_in, first_out), (back_in, back_out), (basis_in, basis_out))
    copies = [pltpu.make_async_copy(src, dst, sems.at[i]) for i, (src, dst) in enumerate(pairs)]
    for copy in copies:
        copy.start()
    proj_out[...] = exact(inv[...], proj_in[...])
    for copy in copies:
        copy.wait()


def solution(mesh):
    n_s, n_t = mesh.shape["series"], mesh.shape["tm"]
    n_z, n_g = n_s // 2, n_s // 4

    def local(traffic, sketch):
        rows, cols = traffic.shape
        k = sketch.shape[1]
        vmem, hbm, anywhere = (pl.BlockSpec(memory_space=m) for m in (pltpu.VMEM, pltpu.HBM, pl.ANY))
        sem = pltpu.SemaphoreType.DMA
        chunk = (k, LANES)
        gram = (k // 2, 2 * k)
        by_rows, by_cols = jax.ShapeDtypeStruct((k, rows), F32), jax.ShapeDtypeStruct((k, cols), F32)
        outs = pl.pallas_call(
            functools.partial(kernel, n_s, n_t),
            out_shape=(by_rows, by_cols, by_rows, by_cols, jax.ShapeDtypeStruct((k, k), F32)),
            in_specs=[hbm, hbm],
            out_specs=(vmem,) * 5,
            scratch_shapes=[
                pltpu.VMEM((rows, cols), BF16),
                pltpu.VMEM((k, cols), F32),
                pltpu.VMEM((3 * k, cols), BF16),
                pltpu.VMEM((2, n_t, *chunk), F32),
                pltpu.VMEM((2, n_t, *chunk), F32),
                pltpu.VMEM((2, n_t, *chunk), F32),
                pltpu.VMEM((2, 2, n_z, *chunk), F32),
                pltpu.VMEM((2, n_z, *chunk), F32),
                pltpu.VMEM((2, n_z, *chunk), F32),
                pltpu.VMEM((2, n_z, *chunk), F32),
                pltpu.VMEM((2, 2, n_z, *chunk), F32),
                pltpu.VMEM((3, k, cols), F32),
                pltpu.VMEM((k, cols), F32),
                pltpu.VMEM((k, rows), F32),
                pltpu.VMEM((k // 2, LANES), F32),
                pltpu.VMEM((k // 2, LANES), F32),
                pltpu.VMEM((3, k, k), F32),
                pltpu.VMEM((k, 2 * k), F32),
                pltpu.VMEM((3, *gram), F32),
                pltpu.VMEM((n_t, *gram), F32),
                pltpu.VMEM((2, n_z, *gram), F32),
                pltpu.VMEM((2, *gram), F32),
                pltpu.VMEM((2, *gram), F32),
                sem((math.isqrt(n_t),)), sem,
                sem((2, 2)), sem((2, 2)), sem((2, 2)), sem((2, 2)),
                sem((2, 2, n_g)), sem((2, 2, n_g)),
                sem((2, 2)), sem((2, 2)), sem((2, 2)), sem((2, 2)), sem((2, 2)), sem((2, 2)),
                sem((3,)), sem((3,)), sem((2,)), sem((2,)),
            ],
            compiler_params=pltpu.CompilerParams(
                collective_id=0, has_side_effects=True, vmem_limit_bytes=48 * 2**20
            ),
            name="range_finder",
        )(traffic, sketch.T)
        first, back, basis, proj = pl.pallas_call(
            finish,
            out_shape=(by_rows, by_cols, by_rows, by_cols),
            in_specs=[anywhere] * 3 + [vmem] * 2,
            out_specs=(anywhere,) * 3 + (vmem,),
            scratch_shapes=[sem((3,))],
            compiler_params=pltpu.CompilerParams(vmem_limit_bytes=8 * 2**20),
            name="finish",
        )(*outs)
        return first.T, back.T, basis.T, proj

    in_specs = (P("series", "tm"), P("tm", None))
    out_specs = (P("series", None), P("tm", None), P("series", None), P(None, "tm"))
    return jax.shard_map(local, mesh=mesh, in_specs=in_specs, out_specs=out_specs, check_vma=False)
```

```python
import functools
import math

import jax
import jax.numpy as jnp
from jax import lax
from jax.experimental import pallas as pl
from jax.experimental.pallas import tpu as pltpu
from jax.sharding import PartitionSpec as P

F32, BF16 = jnp.float32, jnp.bfloat16
HIGHEST = lax.Precision.HIGHEST
MESH = pl.DeviceIdType.MESH
LANES = 128
PANEL = 8
NN = (((1,), (0,)), ((), ()))
NT = (((1,), (1,)), ((), ()))


def far_first(n):
    return sorted(range(n), key=lambda d: (-min(d, n - d), d))


def exact(x, y, dims=NN):
    return lax.dot_general(x, y, dims, precision=HIGHEST, preferred_element_type=F32)


def kernel(
    n_s, n_t, a_hbm, sketch_hbm, first_out, back_out, basis_out, proj_out,
    a, sketch, lhs, tm_part, tm_in, tm_full, z_part, sib_in, z_send, z_in, z_full, flats, back_flat, basis_flat, tm_low, z_low, invs, work,
    g_out, g_pair, g_tm, g_z, g_sum,
    a_sem, s_sem, tm_rs_s, tm_rs_r, tm_ag_s, tm_ag_r, sib_s, sib_r, z_rs_s, z_rs_r, z_ag_s, z_ag_r, fw_s, fw_r,
    gp_s, gp_r, g_s, g_r, gs_s, gs_r,
):
    n_z, n_g = n_s // 2, n_s // 4
    n_x = math.isqrt(n_t)
    n_y = n_t // n_x
    k_all = sketch.shape[0]
    k_half, k_quarter = k_all // 2, k_all // 4
    rows, cols = a.shape
    rows_total, cols_total = rows * n_s, cols * n_t
    s, t = lax.axis_index("series"), lax.axis_index("tm")
    z, core, y, x = s // 2, s % 2, t // n_x, t % n_x
    other = 2 * z + 1 - core
    halves = (pl.ds(0, k_half), pl.ds(k_half, k_half))

    tm_y = {d: (y + d) % n_y for d in range(n_y)}
    tm_x = {d: (x + d) % n_x for d in range(n_x)}
    tm_to = {(dy, dx): tm_y[dy] * n_x + tm_x[dx] for dy in range(n_y) for dx in range(n_x)}
    z_to = {d: (z + d) % n_z for d in range(n_z)}
    z_group = {d: (z // 2 + d) % n_g for d in range(n_g)}
    tm_order = sorted((o for o in tm_to if o != (0, 0)), key=lambda o: -min(o[0], n_y - o[0]) - min(o[1], n_x - o[1]))
    z_order = [d for d in far_first(n_z) if d]

    def remote(src, dst, send, recv, to_s, to_t):
        return pltpu.make_async_remote_copy(
            src_ref=src, dst_ref=dst, send_sem=send, recv_sem=recv, device_id=(to_s, to_t), device_id_type=MESH
        )

    def settle(ref, sem):
        pltpu.make_async_copy(ref, ref, sem).wait()

    barrier = pltpu.get_barrier_semaphore()
    greeted = [(s, tm_to[o]) for o in tm_order] + [(2 * z_to[d] + core, t) for d in z_order] + [(other, t)]
    for device in greeted:
        pl.semaphore_signal(barrier, inc=1, device_id=device, device_id_type=MESH)

    block_rows = n_x * LANES

    def tm_block(dy):
        return pl.ds(pl.multiple_of(tm_y[dy] * block_rows, block_rows), block_rows)

    sketch_copy = pltpu.make_async_copy(sketch_hbm, sketch, s_sem)
    sketch_copy.start()
    a_copies = {dy: pltpu.make_async_copy(a_hbm.at[tm_block(dy), :], a.at[tm_block(dy), :], a_sem.at[dy]) for dy in range(n_y)}
    for dy in far_first(n_y):
        a_copies[dy].start()

    def split(v, h, lanes):
        for term in range(3):
            low = v.astype(BF16)
            lhs[pl.ds((3 * h + term) * k_half, k_half), lanes] = low
            v = v - low.astype(F32)

    def terms(*hs):
        return lhs[pl.ds(3 * hs[0] * k_half, 3 * len(hs) * k_half), :]

    def join(acc):
        return acc[:k_half] + (acc[k_half : 2 * k_half] + acc[2 * k_half : 3 * k_half])

    def tm_product(stage, hs, between=None, ready=None):
        for i, dy in enumerate(far_first(n_y)):
            if ready is not None:
                ready(dy)
            acc = lax.dot_general(terms(*hs), a[tm_block(dy), :], NT, preferred_element_type=F32)
            for h in hs:
                val = join(acc[3 * (h - hs[0]) * k_half :])
                for e in range(n_x):
                    tm_part[stage, tm_y[dy] * n_x + e, halves[h], :] = val[:, e * LANES : (e + 1) * LANES]
                for dx in far_first(n_x):
                    if (dy, dx) != (0, 0):
                        to = tm_to[dy, dx]
                        remote(
                            tm_part.at[stage, to, halves[h], :], tm_in.at[stage, t, halves[h], :],
                            tm_rs_s.at[stage, h], tm_rs_r.at[stage, h], s, to,
                        ).start()
            if between and i == min(between[0], n_y - 1):
                between[1]()

    def tm_sum(stage, h):
        settle(tm_in.at[stage, pl.ds(0, n_t - 1), halves[h], :], tm_rs_r.at[stage, h])
        tm_in[stage, t, halves[h], :] = tm_part[stage, t, halves[h], :]
        total = tm_in[stage, 0, halves[h], :]
        for i in range(1, n_t):
            total = total + tm_in[stage, i, halves[h], :]
        return total

    def tm_gather(stage, h, chunk):
        tm_full[stage, t, halves[h], :] = chunk
        mine = tm_full.at[stage, t, halves[h], :]
        for o in tm_order:
            remote(mine, mine, tm_ag_s.at[stage, h], tm_ag_r.at[stage, h], s, tm_to[o]).start()

    def tm_take(stage, h, flat):
        settle(tm_full.at[stage, pl.ds(0, n_t - 1), halves[h], :], tm_ag_r.at[stage, h])
        for c in range(n_t):
            lanes = pl.ds(c * LANES, LANES)
            v = tm_full[stage, c, halves[h], :]
            flat[halves[h], lanes] = v
            split(v, h, lanes)

    def z_pair(dg):
        return pl.ds(2 * z_group[dg], 2)

    def sibling(stage, h, dg):
        return remote(
            z_part.at[stage, 1 - core, z_pair(dg), halves[h], :], sib_in.at[stage, z_pair(dg), halves[h], :],
            sib_s.at[stage, h, dg], sib_r.at[stage, h, dg], other, t,
        )

    def z_both(stage, h, dg):
        sibling(stage, h, dg).wait_recv()
        pair = z_pair(dg)
        z_send[stage, pair, halves[h], :] = z_part[stage, core, pair, halves[h], :] + sib_in[stage, pair, halves[h], :]
        tos = [2 * z_group[dg] + e for e in range(2)] if dg else [4 * (z // 2) + 1 - z]
        for to in tos:
            remote(
                z_send.at[stage, to, halves[h], :], z_in.at[stage, z, halves[h], :],
                z_rs_s.at[stage, h], z_rs_r.at[stage, h], 2 * to + core, t,
            ).start()

    def z_product(stage, h, between=None):
        before = None
        for i, dg in enumerate(far_first(n_g)):
            block = pl.ds(pl.multiple_of(z_group[dg] * 4 * LANES, 4 * LANES), 4 * LANES)
            acc = lax.dot_general(terms(h), a[:, block], NN, preferred_element_type=F32)
            val = join(acc)
            for e in range(4):
                z_part[stage, e % 2, 2 * z_group[dg] + e // 2, halves[h], :] = val[:, e * LANES : (e + 1) * LANES]
            sibling(stage, h, dg).start()
            if before is not None:
                z_both(stage, h, before)
            before = dg
            if between and i == min(between[0], n_g - 1):
                between[1]()

    def z_sum(stage, h):
        settle(z_in.at[stage, pl.ds(0, n_z - 1), halves[h], :], z_rs_r.at[stage, h])
        z_in[stage, z, halves[h], :] = z_send[stage, z, halves[h], :]
        total = z_in[stage, 0, halves[h], :]
        for i in range(1, n_z):
            total = total + z_in[stage, i, halves[h], :]
        return total

    def z_gather(stage, h, chunk):
        z_full[stage, core, z, halves[h], :] = chunk
        mine = z_full.at[stage, core, z, halves[h], :]
        for d in z_order:
            remote(mine, mine, z_ag_s.at[stage, h], z_ag_r.at[stage, h], 2 * z_to[d] + core, t).start()

    def z_forward(stage, h):
        settle(z_full.at[stage, core, pl.ds(0, n_z - 1), halves[h], :], z_ag_r.at[stage, h])
        mine = z_full.at[stage, core, :, halves[h], :]
        remote(mine, mine, fw_s.at[stage, h], fw_r.at[stage, h], other, t).start()

    def z_take(stage, h, flat, again=True):
        settle(z_full.at[stage, core, :, halves[h], :], fw_r.at[stage, h])
        for c in range(n_s):
            lanes = pl.ds(c * LANES, LANES)
            v = z_full[stage, c % 2, c // 2, halves[h], :]
            flat[halves[h], lanes] = v
            if again:
                split(v, h, lanes)

    def pack(flat, out):
        gram = exact(flat[...], flat[...], NT)
        for c in range(2):
            out[c, :, :k_all] = gram[c * k_quarter : (c + 1) * k_quarter]
            out[c, :, k_all:] = gram[k_half + c * k_quarter : k_half + (c + 1) * k_quarter]

    def gram_swap(i, total):
        g_sum[i, core] = total
        mine = g_sum.at[i, core]
        remote(mine, mine, gs_s.at[i], gs_r.at[i], other, t).start()

    def gram_end(i):
        settle(g_sum.at[i, core], gs_r.at[i])
        return g_sum[i]

    def gram_z_send(i, flat):
        pack(flat, g_out.at[i])
        remote(g_out.at[i, 1 - core], g_pair.at[i // 2], gp_s.at[i // 2], gp_r.at[i // 2], other, t).start()

    def gram_z_pair(i):
        b = i // 2
        settle(g_pair.at[b], gp_r.at[b])
        g_z[b, z] = g_out[i, core] + g_pair[b]
        mine = g_z.at[b, z]
        for d in z_order:
            remote(mine, mine, g_s.at[i], g_r.at[i], 2 * z_to[d] + core, t).start()

    def gram_z_middle(i):
        b = i // 2
        settle(g_z.at[b, pl.ds(0, n_z - 1)], g_r.at[i])
        total = g_z[b, 0]
        for k in range(1, n_z):
            total = total + g_z[b, k]
        gram_swap(i, total)

    def gram_tm_send(i, flat):
        pack(flat, g_out.at[i])
        g_tm[t] = g_out[i, core]
        mine = g_tm.at[t]
        for o in tm_order:
            remote(mine, mine, g_s.at[i], g_r.at[i], s, tm_to[o]).start()

    def gram_tm_middle(i):
        settle(g_tm.at[pl.ds(0, n_t - 1)], g_r.at[i])
        total = g_tm[0]
        for k in range(1, n_t):
            total = total + g_tm[k]
        gram_swap(i, total)

    def invert(i, packed):
        lane = lax.broadcasted_iota(jnp.int32, (k_all, 2 * k_all), 1)
        row = lax.broadcasted_iota(jnp.int32, (k_all, 2 * k_all), 0)
        work[...] = jnp.where(lane == row + k_all, 1.0, 0.0).astype(F32)
        for c in range(2):
            work[pl.ds(c * k_quarter, k_quarter), :k_all] = packed[c, :, :k_all]
            work[pl.ds(k_half + c * k_quarter, k_quarter), :k_all] = packed[c, :, k_all:]
        v = work[...]
        for j in range(0, k_all, PANEL):
            col = [jnp.broadcast_to(v[:, j + m : j + m + 1], v.shape) for m in range(PANEL)]
            line = [v[j + m : j + m + 1, :] for m in range(PANEL)]
            for m in range(PANEL):
                factor = jnp.where(row > j + m, col[m] * (1.0 / col[m][j + m : j + m + 1, :]), 0.0)
                for n in range(m + 1, PANEL):
                    line[n] = line[n] - factor[j + n : j + n + 1, :] * line[m]
                    col[n] = col[n] - factor * col[n][j + m : j + m + 1, :]
                v = v - factor * line[m]
        diag = jnp.sum(jnp.where(lane == row, v, 0.0), axis=1, keepdims=True)
        invs[i] = (v * lax.rsqrt(diag))[:, k_all:]

    def apply_a(i, low):
        return exact(invs[i, :k_half, :k_half], low)

    def apply_b(i, low, high):
        return exact(invs[i, k_half:, :k_half], low) + exact(invs[i, k_half:, k_half:], high)

    sketch_copy.wait()
    for h in range(2):
        split(sketch[halves[h], :], h, slice(None))

    def ready(dy):
        a_copies[dy].wait()
        if dy == far_first(n_y)[0]:
            pl.semaphore_wait(barrier, len(greeted))

    tm_product(0, (0, 1), ready=ready)
    for h in range(2):
        tm_gather(0, h, tm_sum(0, h))
    tm_take(0, 0, flats.at[0])

    z_product(0, 0)
    tm_take(0, 1, flats.at[0])
    z_both(0, 0, 0)
    z_product(0, 1, (2, lambda: z_gather(0, 0, z_sum(0, 0))))
    z_both(0, 1, 0)
    gram_z_send(0, flats.at[0])
    gram_z_pair(0)
    z_gather(0, 1, z_sum(0, 1))
    z_forward(0, 0)
    z_take(0, 0, flats.at[1])

    def last_of_back():
        gram_z_middle(0)
        z_forward(0, 1)

    tm_product(1, (0,), (2, last_of_back))
    invert(0, gram_end(0))
    z_take(0, 1, flats.at[1])

    def tm_first_half():
        tm_low[...] = tm_sum(1, 0)
        tm_gather(1, 0, apply_a(0, tm_low[...]))

    tm_product(1, (1,), (0, tm_first_half))
    back_flat[...] = exact(invs[0], flats[1])
    gram_tm_send(1, back_flat)
    first_out[...] = (rows_total**0.5) * exact(invs[0], flats[0])
    tm_gather(1, 1, apply_b(0, tm_low[...], tm_sum(1, 1)))
    tm_take(1, 0, flats.at[2])

    z_product(1, 0, (2, lambda: gram_tm_middle(1)))
    z_both(1, 0, 0)
    invert(1, gram_end(1))
    tm_take(1, 1, flats.at[2])

    def z_first_half():
        z_low[...] = z_sum(1, 0)
        z_gather(1, 0, apply_a(1, z_low[...]))

    z_product(1, 1, (1, z_first_half))
    z_both(1, 1, 0)
    basis_flat[...] = exact(invs[1], flats[2])
    gram_z_send(2, basis_flat)
    gram_z_pair(2)
    z_gather(1, 1, apply_b(1, z_low[...], z_sum(1, 1)))
    back_out[...] = (cols_total**0.5) * exact(invs[1], back_flat[...])
    z_forward(1, 0)
    gram_z_middle(2)
    invert(2, gram_end(2))
    z_forward(1, 1)
    basis_out[...] = (rows_total**0.5) * exact(invs[2], basis_flat[...])
    z_take(1, 0, flats.at[3], again=False)
    proj_out[:k_half, :] = exact(invs[2, :k_half, :k_half], flats[3, :k_half, :])
    z_take(1, 1, flats.at[3], again=False)
    proj_out[k_half:, :] = exact(invs[2, k_half:, :], flats[3])

    for stage in range(2):
        for h in range(2):
            settle(tm_in.at[stage, pl.ds(0, n_t - 1), halves[h], :], tm_rs_s.at[stage, h])
            settle(z_in.at[stage, pl.ds(0, n_z - 1), halves[h], :], z_rs_s.at[stage, h])
            settle(tm_full.at[stage, pl.ds(0, n_t - 1), halves[h], :], tm_ag_s.at[stage, h])
            settle(z_full.at[stage, core, pl.ds(0, n_z - 1), halves[h], :], z_ag_s.at[stage, h])
            settle(z_full.at[stage, core, :, halves[h], :], fw_s.at[stage, h])
            for dg in range(n_g):
                settle(sib_in.at[stage, pl.ds(0, 2), halves[h], :], sib_s.at[stage, h, dg])
        settle(g_z.at[stage, pl.ds(0, n_z - 1)], g_s.at[2 * stage])
        settle(g_pair.at[stage], gp_s.at[stage])
    settle(g_tm.at[pl.ds(0, n_t - 1)], g_s.at[1])
    for i in range(3):
        settle(g_sum.at[i, core], gs_s.at[i])


def finish(*refs):
    sems = refs[-1]
    copies = [pltpu.make_async_copy(refs[i], refs[4 + i], sems.at[i]) for i in range(4)]
    for copy in copies:
        copy.start()
    for copy in copies:
        copy.wait()


def solution(mesh):
    n_s, n_t = mesh.shape["series"], mesh.shape["tm"]
    n_z, n_g = n_s // 2, n_s // 4

    def local(traffic, sketch):
        rows, cols = traffic.shape
        k = sketch.shape[1]
        vmem, hbm, anywhere = (pl.BlockSpec(memory_space=m) for m in (pltpu.VMEM, pltpu.HBM, pl.ANY))
        sem = pltpu.SemaphoreType.DMA
        chunk = (k, LANES)
        gram = (k // 4, 2 * k)
        by_rows, by_cols = jax.ShapeDtypeStruct((k, rows), F32), jax.ShapeDtypeStruct((k, cols), F32)
        outs = pl.pallas_call(
            functools.partial(kernel, n_s, n_t),
            out_shape=(by_rows, by_cols, by_rows, by_cols),
            in_specs=[hbm, hbm],
            out_specs=(vmem,) * 4,
            scratch_shapes=[
                pltpu.VMEM((rows, cols), BF16),
                pltpu.VMEM((k, cols), F32),
                pltpu.VMEM((3 * k, cols), BF16),
                pltpu.VMEM((2, n_t, *chunk), F32),
                pltpu.VMEM((2, n_t, *chunk), F32),
                pltpu.VMEM((2, n_t, *chunk), F32),
                pltpu.VMEM((2, 2, n_z, *chunk), F32),
                pltpu.VMEM((2, n_z, *chunk), F32),
                pltpu.VMEM((2, n_z, *chunk), F32),
                pltpu.VMEM((2, n_z, *chunk), F32),
                pltpu.VMEM((2, 2, n_z, *chunk), F32),
                pltpu.VMEM((4, k, cols), F32),
                pltpu.VMEM((k, cols), F32),
                pltpu.VMEM((k, rows), F32),
                pltpu.VMEM((k // 2, LANES), F32),
                pltpu.VMEM((k // 2, LANES), F32),
                pltpu.VMEM((3, k, k), F32),
                pltpu.VMEM((k, 2 * k), F32),
                pltpu.VMEM((3, 2, *gram), F32),
                pltpu.VMEM((2, *gram), F32),
                pltpu.VMEM((n_t, *gram), F32),
                pltpu.VMEM((2, n_z, *gram), F32),
                pltpu.VMEM((3, 2, *gram), F32),
                sem((math.isqrt(n_t),)), sem,
                sem((2, 2)), sem((2, 2)), sem((2, 2)), sem((2, 2)),
                sem((2, 2, n_g)), sem((2, 2, n_g)),
                sem((2, 2)), sem((2, 2)), sem((2, 2)), sem((2, 2)), sem((2, 2)), sem((2, 2)),
                sem((2,)), sem((2,)), sem((3,)), sem((3,)), sem((3,)), sem((3,)),
            ],
            compiler_params=pltpu.CompilerParams(
                collective_id=0, has_side_effects=True, vmem_limit_bytes=48 * 2**20
            ),
            name="range_finder",
        )(traffic, pltpu.with_memory_space_constraint(sketch.T, pltpu.HBM))
        first, back, basis, proj = pl.pallas_call(
            finish,
            out_shape=(by_rows, by_cols, by_rows, by_cols),
            in_specs=[anywhere] * 4,
            out_specs=(anywhere,) * 4,
            scratch_shapes=[sem((4,))],
            compiler_params=pltpu.CompilerParams(vmem_limit_bytes=8 * 2**20),
            name="finish",
        )(*outs)
        return first.T, back.T, basis.T, proj

    in_specs = (P("series", "tm"), P("tm", None))
    out_specs = (P("series", None), P("tm", None), P("series", None), P(None, "tm"))
    return jax.shard_map(local, mesh=mesh, in_specs=in_specs, out_specs=out_specs, check_vma=False)
```

```python
import functools
import math

import jax
import jax.numpy as jnp
from jax import lax
from jax.experimental import pallas as pl
from jax.experimental.pallas import tpu as pltpu
from jax.sharding import PartitionSpec as P

F32, BF16 = jnp.float32, jnp.bfloat16
HIGHEST = lax.Precision.HIGHEST
MESH = pl.DeviceIdType.MESH
LANES = 128
PANEL = 16
NN = (((1,), (0,)), ((), ()))
NT = (((1,), (1,)), ((), ()))


def far_first(n):
    return sorted(range(n), key=lambda d: (-min(d, n - d), d))


def exact(x, y, dims=NN):
    return lax.dot_general(x, y, dims, precision=HIGHEST, preferred_element_type=F32)


def kernel(
    n_s, n_t, a_hbm, sketch_hbm, first_out, back_out, basis_out, proj_out,
    a, sketch, lhs, tm_part, tm_in, tm_full, z_part, sib_in, z_send, z_in, z_full, flats, back_flat, basis_flat, tm_low, z_low, invs, work,
    g_out, g_pair, g_tm, g_z, g_sum,
    a_sem, s_sem, tm_rs_s, tm_rs_r, tm_ag_s, tm_ag_r, sib_s, sib_r, z_rs_s, z_rs_r, z_ag_s, z_ag_r, fw_s, fw_r,
    gp_s, gp_r, g_s, g_r, gs_s, gs_r,
):
    n_z, n_g = n_s // 2, n_s // 4
    n_x = math.isqrt(n_t)
    n_y = n_t // n_x
    k_all = sketch.shape[0]
    k_half, k_quarter = k_all // 2, k_all // 4
    rows, cols = a.shape
    rows_total, cols_total = rows * n_s, cols * n_t
    s, t = lax.axis_index("series"), lax.axis_index("tm")
    z, core, y, x = s // 2, s % 2, t // n_x, t % n_x
    other = 2 * z + 1 - core
    halves = (pl.ds(0, k_half), pl.ds(k_half, k_half))

    tm_y = {d: (y + d) % n_y for d in range(n_y)}
    tm_x = {d: (x + d) % n_x for d in range(n_x)}
    tm_to = {(dy, dx): tm_y[dy] * n_x + tm_x[dx] for dy in range(n_y) for dx in range(n_x)}
    z_to = {d: (z + d) % n_z for d in range(n_z)}
    z_group = {d: (z // 2 + d) % n_g for d in range(n_g)}
    tm_order = sorted((o for o in tm_to if o != (0, 0)), key=lambda o: -min(o[0], n_y - o[0]) - min(o[1], n_x - o[1]))
    z_order = [d for d in far_first(n_z) if d]

    def remote(src, dst, send, recv, to_s, to_t):
        return pltpu.make_async_remote_copy(
            src_ref=src, dst_ref=dst, send_sem=send, recv_sem=recv, device_id=(to_s, to_t), device_id_type=MESH
        )

    def settle(ref, sem):
        pltpu.make_async_copy(ref, ref, sem).wait()

    barrier = pltpu.get_barrier_semaphore()
    greeted = [(s, tm_to[o]) for o in tm_order] + [(2 * z_to[d] + core, t) for d in z_order] + [(other, t)]
    for device in greeted:
        pl.semaphore_signal(barrier, inc=1, device_id=device, device_id_type=MESH)

    block_rows = n_x * LANES

    def tm_block(dy):
        return pl.ds(pl.multiple_of(tm_y[dy] * block_rows, block_rows), block_rows)

    sketch_copy = pltpu.make_async_copy(sketch_hbm, sketch, s_sem)
    sketch_copy.start()
    a_copies = {dy: pltpu.make_async_copy(a_hbm.at[tm_block(dy), :], a.at[tm_block(dy), :], a_sem.at[dy]) for dy in range(n_y)}
    for dy in far_first(n_y):
        a_copies[dy].start()

    def split(v, h, lanes):
        for term in range(3):
            low = v.astype(BF16)
            lhs[pl.ds((3 * h + term) * k_half, k_half), lanes] = low
            v = v - low.astype(F32)

    def terms(*hs):
        return lhs[pl.ds(3 * hs[0] * k_half, 3 * len(hs) * k_half), :]

    def join(acc):
        return acc[:k_half] + (acc[k_half : 2 * k_half] + acc[2 * k_half : 3 * k_half])

    def tm_multiply(stage, hs, dy):
        acc = lax.dot_general(terms(*hs), a[tm_block(dy), :], NT, preferred_element_type=F32)
        for h in hs:
            val = join(acc[3 * (h - hs[0]) * k_half :])
            for e in range(n_x):
                tm_part[stage, tm_y[dy] * n_x + e, halves[h], :] = val[:, e * LANES : (e + 1) * LANES]

    def tm_send(stage, h, dy):
        for dx in far_first(n_x):
            if (dy, dx) != (0, 0):
                to = tm_to[dy, dx]
                remote(
                    tm_part.at[stage, to, halves[h], :], tm_in.at[stage, t, halves[h], :],
                    tm_rs_s.at[stage, h], tm_rs_r.at[stage, h], s, to,
                ).start()

    def tm_product(stage, h, between=None):
        for i, dy in enumerate(far_first(n_y)):
            tm_multiply(stage, (h,), dy)
            tm_send(stage, h, dy)
            if between and i == min(between[0], n_y - 1):
                between[1]()

    def tm_sum(stage, h):
        settle(tm_in.at[stage, pl.ds(0, n_t - 1), halves[h], :], tm_rs_r.at[stage, h])
        tm_in[stage, t, halves[h], :] = tm_part[stage, t, halves[h], :]
        total = tm_in[stage, 0, halves[h], :]
        for i in range(1, n_t):
            total = total + tm_in[stage, i, halves[h], :]
        return total

    def tm_gather(stage, h, chunk):
        tm_full[stage, t, halves[h], :] = chunk
        mine = tm_full.at[stage, t, halves[h], :]
        for o in tm_order:
            remote(mine, mine, tm_ag_s.at[stage, h], tm_ag_r.at[stage, h], s, tm_to[o]).start()

    def tm_take(stage, h, flat):
        settle(tm_full.at[stage, pl.ds(0, n_t - 1), halves[h], :], tm_ag_r.at[stage, h])
        for c in range(n_t):
            lanes = pl.ds(c * LANES, LANES)
            v = tm_full[stage, c, halves[h], :]
            flat[halves[h], lanes] = v
            split(v, h, lanes)

    def z_pair(dg):
        return pl.ds(2 * z_group[dg], 2)

    def sibling(stage, h, dg):
        return remote(
            z_part.at[stage, 1 - core, z_pair(dg), halves[h], :], sib_in.at[stage, z_pair(dg), halves[h], :],
            sib_s.at[stage, h, dg], sib_r.at[stage, h, dg], other, t,
        )

    def z_both(stage, h, dg):
        sibling(stage, h, dg).wait_recv()
        pair = z_pair(dg)
        z_send[stage, pair, halves[h], :] = z_part[stage, core, pair, halves[h], :] + sib_in[stage, pair, halves[h], :]
        tos = [2 * z_group[dg] + e for e in range(2)] if dg else [4 * (z // 2) + 1 - z]
        for to in tos:
            remote(
                z_send.at[stage, to, halves[h], :], z_in.at[stage, z, halves[h], :],
                z_rs_s.at[stage, h], z_rs_r.at[stage, h], 2 * to + core, t,
            ).start()

    def z_product(stage, h, between=None):
        before = None
        for i, dg in enumerate(far_first(n_g)):
            block = pl.ds(pl.multiple_of(z_group[dg] * 4 * LANES, 4 * LANES), 4 * LANES)
            acc = lax.dot_general(terms(h), a[:, block], NN, preferred_element_type=F32)
            val = join(acc)
            for e in range(4):
                z_part[stage, e % 2, 2 * z_group[dg] + e // 2, halves[h], :] = val[:, e * LANES : (e + 1) * LANES]
            sibling(stage, h, dg).start()
            if before is not None:
                z_both(stage, h, before)
            before = dg
            if between and i == min(between[0], n_g - 1):
                between[1]()

    def z_sum(stage, h):
        settle(z_in.at[stage, pl.ds(0, n_z - 1), halves[h], :], z_rs_r.at[stage, h])
        z_in[stage, z, halves[h], :] = z_send[stage, z, halves[h], :]
        total = z_in[stage, 0, halves[h], :]
        for i in range(1, n_z):
            total = total + z_in[stage, i, halves[h], :]
        return total

    def z_gather(stage, h, chunk):
        z_full[stage, core, z, halves[h], :] = chunk
        mine = z_full.at[stage, core, z, halves[h], :]
        for d in z_order:
            remote(mine, mine, z_ag_s.at[stage, h], z_ag_r.at[stage, h], 2 * z_to[d] + core, t).start()

    def z_forward(stage, h):
        settle(z_full.at[stage, core, pl.ds(0, n_z - 1), halves[h], :], z_ag_r.at[stage, h])
        mine = z_full.at[stage, core, :, halves[h], :]
        remote(mine, mine, fw_s.at[stage, h], fw_r.at[stage, h], other, t).start()

    def z_take(stage, h, flat, again=True):
        settle(z_full.at[stage, core, :, halves[h], :], fw_r.at[stage, h])
        for c in range(n_s):
            lanes = pl.ds(c * LANES, LANES)
            v = z_full[stage, c % 2, c // 2, halves[h], :]
            flat[halves[h], lanes] = v
            if again:
                split(v, h, lanes)

    def pack(flat, out):
        gram = exact(flat[...], flat[...], NT)
        for c in range(2):
            out[c, :, :k_all] = gram[c * k_quarter : (c + 1) * k_quarter]
            out[c, :, k_all:] = gram[k_half + c * k_quarter : k_half + (c + 1) * k_quarter]

    def gram_swap(i, total):
        g_sum[i, core] = total
        mine = g_sum.at[i, core]
        remote(mine, mine, gs_s.at[i], gs_r.at[i], other, t).start()

    def gram_end(i):
        settle(g_sum.at[i, core], gs_r.at[i])
        return g_sum[i]

    def gram_z_send(i, flat):
        pack(flat, g_out.at[i])
        remote(g_out.at[i, 1 - core], g_pair.at[i // 2], gp_s.at[i // 2], gp_r.at[i // 2], other, t).start()

    def gram_z_pair(i):
        b = i // 2
        settle(g_pair.at[b], gp_r.at[b])
        g_z[b, z] = g_out[i, core] + g_pair[b]
        mine = g_z.at[b, z]
        for d in z_order:
            remote(mine, mine, g_s.at[i], g_r.at[i], 2 * z_to[d] + core, t).start()

    def gram_z_middle(i):
        b = i // 2
        settle(g_z.at[b, pl.ds(0, n_z - 1)], g_r.at[i])
        total = g_z[b, 0]
        for k in range(1, n_z):
            total = total + g_z[b, k]
        gram_swap(i, total)

    def gram_tm_send(i, flat):
        pack(flat, g_out.at[i])
        g_tm[t] = g_out[i, core]
        mine = g_tm.at[t]
        for o in tm_order:
            remote(mine, mine, g_s.at[i], g_r.at[i], s, tm_to[o]).start()

    def gram_tm_middle(i):
        settle(g_tm.at[pl.ds(0, n_t - 1)], g_r.at[i])
        total = g_tm[0]
        for k in range(1, n_t):
            total = total + g_tm[k]
        gram_swap(i, total)

    def invert(i, packed):
        lane = lax.broadcasted_iota(jnp.int32, (k_all, 2 * k_all), 1)
        row = lax.broadcasted_iota(jnp.int32, (k_all, 2 * k_all), 0)
        work[...] = jnp.where(lane == row + k_all, 1.0, 0.0).astype(F32)
        for c in range(2):
            work[pl.ds(c * k_quarter, k_quarter), :k_all] = packed[c, :, :k_all]
            work[pl.ds(k_half + c * k_quarter, k_quarter), :k_all] = packed[c, :, k_all:]
        v = work[...]
        for j in range(0, k_all, PANEL):
            below = lax.broadcasted_iota(jnp.int32, v.shape, 0)
            col = [jnp.broadcast_to(v[:, j + m : j + m + 1], v.shape) for m in range(PANEL)]
            line = [v[m : m + 1, :] for m in range(PANEL)]
            for m in range(PANEL):
                factor = jnp.where(below > m, col[m] * (1.0 / col[m][m : m + 1, :]), 0.0)
                for n in range(m + 1, PANEL):
                    line[n] = line[n] - factor[n : n + 1, :] * line[m]
                    col[n] = col[n] - factor * col[n][m : m + 1, :]
                v = v - factor * line[m]
            done, v = v[:PANEL], v[PANEL:]
            mine = (lane == row + j)[:PANEL]
            diag = jnp.sum(jnp.where(mine, done, 0.0), axis=1, keepdims=True)
            invs[i, j : j + PANEL, :] = (done * lax.rsqrt(diag))[:, k_all:]

    def apply_a(i, low):
        return exact(invs[i, :k_half, :k_half], low)

    def apply_b(i, low, high):
        return exact(invs[i, k_half:, :k_half], low) + exact(invs[i, k_half:, k_half:], high)

    sketch_copy.wait()
    for h in range(2):
        split(sketch[halves[h], :], h, slice(None))

    for dy in far_first(n_y):
        a_copies[dy].wait()
        tm_multiply(0, (0, 1), dy)
    pl.semaphore_wait(barrier, len(greeted))
    for h in range(2):
        for dy in far_first(n_y):
            tm_send(0, h, dy)
    for h in range(2):
        tm_gather(0, h, tm_sum(0, h))
    tm_take(0, 0, flats.at[0])

    z_product(0, 0)
    tm_take(0, 1, flats.at[0])
    z_both(0, 0, 0)
    z_product(0, 1)
    z_both(0, 1, 0)
    z_gather(0, 0, z_sum(0, 0))
    gram_z_send(0, flats.at[0])
    gram_z_pair(0)
    z_gather(0, 1, z_sum(0, 1))
    z_forward(0, 0)
    z_take(0, 0, flats.at[1])
    gram_z_middle(0)

    tm_product(1, 0, (2, lambda: z_forward(0, 1)))
    invert(0, gram_end(0))
    z_take(0, 1, flats.at[1])
    tm_product(1, 1)
    tm_low[...] = tm_sum(1, 0)
    tm_gather(1, 0, apply_a(0, tm_low[...]))
    back_flat[...] = exact(invs[0], flats[1])
    gram_tm_send(1, back_flat)
    first_out[...] = (rows_total**0.5) * exact(invs[0], flats[0])
    tm_gather(1, 1, apply_b(0, tm_low[...], tm_sum(1, 1)))
    tm_take(1, 0, flats.at[2])

    z_product(1, 0, (1, lambda: gram_tm_middle(1)))
    z_both(1, 0, 0)
    invert(1, gram_end(1))
    tm_take(1, 1, flats.at[2])
    z_product(1, 1)
    z_both(1, 1, 0)
    z_low[...] = z_sum(1, 0)
    z_gather(1, 0, apply_a(1, z_low[...]))
    basis_flat[...] = exact(invs[1], flats[2])
    gram_z_send(2, basis_flat)
    gram_z_pair(2)
    z_gather(1, 1, apply_b(1, z_low[...], z_sum(1, 1)))
    back_out[...] = (cols_total**0.5) * exact(invs[1], back_flat[...])
    z_forward(1, 0)
    gram_z_middle(2)
    invert(2, gram_end(2))
    z_forward(1, 1)
    basis_out[...] = (rows_total**0.5) * exact(invs[2], basis_flat[...])
    z_take(1, 0, flats.at[3], again=False)
    proj_out[:k_half, :] = exact(invs[2, :k_half, :k_half], flats[3, :k_half, :])
    z_take(1, 1, flats.at[3], again=False)
    proj_out[k_half:, :] = exact(invs[2, k_half:, :], flats[3])

    for stage in range(2):
        for h in range(2):
            settle(tm_in.at[stage, pl.ds(0, n_t - 1), halves[h], :], tm_rs_s.at[stage, h])
            settle(z_in.at[stage, pl.ds(0, n_z - 1), halves[h], :], z_rs_s.at[stage, h])
            settle(tm_full.at[stage, pl.ds(0, n_t - 1), halves[h], :], tm_ag_s.at[stage, h])
            settle(z_full.at[stage, core, pl.ds(0, n_z - 1), halves[h], :], z_ag_s.at[stage, h])
            settle(z_full.at[stage, core, :, halves[h], :], fw_s.at[stage, h])
            for dg in range(n_g):
                settle(sib_in.at[stage, pl.ds(0, 2), halves[h], :], sib_s.at[stage, h, dg])
        settle(g_z.at[stage, pl.ds(0, n_z - 1)], g_s.at[2 * stage])
        settle(g_pair.at[stage], gp_s.at[stage])
    settle(g_tm.at[pl.ds(0, n_t - 1)], g_s.at[1])
    for i in range(3):
        settle(g_sum.at[i, core], gs_s.at[i])


def finish(*refs):
    sems = refs[-1]
    copies = [pltpu.make_async_copy(refs[i], refs[4 + i], sems.at[i]) for i in range(4)]
    for copy in copies:
        copy.start()
    for copy in copies:
        copy.wait()


def solution(mesh):
    n_s, n_t = mesh.shape["series"], mesh.shape["tm"]
    n_z, n_g = n_s // 2, n_s // 4

    def local(traffic, sketch):
        rows, cols = traffic.shape
        k = sketch.shape[1]
        vmem, hbm, anywhere = (pl.BlockSpec(memory_space=m) for m in (pltpu.VMEM, pltpu.HBM, pl.ANY))
        sem = pltpu.SemaphoreType.DMA
        chunk = (k, LANES)
        gram = (k // 4, 2 * k)
        by_rows, by_cols = jax.ShapeDtypeStruct((k, rows), F32), jax.ShapeDtypeStruct((k, cols), F32)
        outs = pl.pallas_call(
            functools.partial(kernel, n_s, n_t),
            out_shape=(by_rows, by_cols, by_rows, by_cols),
            in_specs=[hbm, hbm],
            out_specs=(vmem,) * 4,
            scratch_shapes=[
                pltpu.VMEM((rows, cols), BF16),
                pltpu.VMEM((k, cols), F32),
                pltpu.VMEM((3 * k, cols), BF16),
                pltpu.VMEM((2, n_t, *chunk), F32),
                pltpu.VMEM((2, n_t, *chunk), F32),
                pltpu.VMEM((2, n_t, *chunk), F32),
                pltpu.VMEM((2, 2, n_z, *chunk), F32),
                pltpu.VMEM((2, n_z, *chunk), F32),
                pltpu.VMEM((2, n_z, *chunk), F32),
                pltpu.VMEM((2, n_z, *chunk), F32),
                pltpu.VMEM((2, 2, n_z, *chunk), F32),
                pltpu.VMEM((4, k, cols), F32),
                pltpu.VMEM((k, cols), F32),
                pltpu.VMEM((k, rows), F32),
                pltpu.VMEM((k // 2, LANES), F32),
                pltpu.VMEM((k // 2, LANES), F32),
                pltpu.VMEM((3, k, k), F32),
                pltpu.VMEM((k, 2 * k), F32),
                pltpu.VMEM((3, 2, *gram), F32),
                pltpu.VMEM((2, *gram), F32),
                pltpu.VMEM((n_t, *gram), F32),
                pltpu.VMEM((2, n_z, *gram), F32),
                pltpu.VMEM((3, 2, *gram), F32),
                sem((math.isqrt(n_t),)), sem,
                sem((2, 2)), sem((2, 2)), sem((2, 2)), sem((2, 2)),
                sem((2, 2, n_g)), sem((2, 2, n_g)),
                sem((2, 2)), sem((2, 2)), sem((2, 2)), sem((2, 2)), sem((2, 2)), sem((2, 2)),
                sem((2,)), sem((2,)), sem((3,)), sem((3,)), sem((3,)), sem((3,)),
            ],
            compiler_params=pltpu.CompilerParams(
                collective_id=0, has_side_effects=True, vmem_limit_bytes=48 * 2**20
            ),
            name="range_finder",
        )(traffic, pltpu.with_memory_space_constraint(sketch.T, pltpu.HBM))
        first, back, basis, proj = pl.pallas_call(
            finish,
            out_shape=(by_rows, by_cols, by_rows, by_cols),
            in_specs=[anywhere] * 4,
            out_specs=(anywhere,) * 4,
            scratch_shapes=[sem((4,))],
            compiler_params=pltpu.CompilerParams(vmem_limit_bytes=8 * 2**20),
            name="finish",
        )(*outs)
        return first.T, back.T, basis.T, proj

    in_specs = (P("series", "tm"), P("tm", None))
    out_specs = (P("series", None), P("tm", None), P("series", None), P(None, "tm"))
    return jax.shard_map(local, mesh=mesh, in_specs=in_specs, out_specs=out_specs, check_vma=False)
```

```python
import functools
import math

import jax
import jax.numpy as jnp
from jax import lax
from jax.experimental import pallas as pl
from jax.experimental.pallas import tpu as pltpu
from jax.sharding import PartitionSpec as P

F32, BF16 = jnp.float32, jnp.bfloat16
HIGHEST = lax.Precision.HIGHEST
MESH = pl.DeviceIdType.MESH
LANES = 128
PANEL = 16
NN = (((1,), (0,)), ((), ()))
NT = (((1,), (1,)), ((), ()))


def far_first(n):
    return sorted(range(n), key=lambda d: (-min(d, n - d), d))


def exact(x, y, dims=NN):
    return lax.dot_general(x, y, dims, precision=HIGHEST, preferred_element_type=F32)


def kernel(
    n_s, n_t, a_hbm, sketch_hbm, first_out, back_out, basis_out, proj_out,
    a, a_turned, sketch, lhs, tm_part, tm_in, tm_full, z_part, sib_in, z_send, z_in, z_full, flats, back_flat, basis_flat, tm_low, z_low, invs, work,
    g_out, g_pair, g_tm, g_z, g_sum,
    a_sem, s_sem, tm_rs_s, tm_rs_r, tm_ag_s, tm_ag_r, sib_s, sib_r, z_rs_s, z_rs_r, z_ag_s, z_ag_r, fw_s, fw_r,
    gp_s, gp_r, g_s, g_r, gs_s, gs_r,
):
    n_z, n_g = n_s // 2, n_s // 4
    n_x = math.isqrt(n_t)
    n_y = n_t // n_x
    k_all = sketch.shape[0]
    k_half, k_quarter = k_all // 2, k_all // 4
    rows, cols = a.shape
    rows_total, cols_total = rows * n_s, cols * n_t
    s, t = lax.axis_index("series"), lax.axis_index("tm")
    z, core, y, x = s // 2, s % 2, t // n_x, t % n_x
    other = 2 * z + 1 - core
    halves = (pl.ds(0, k_half), pl.ds(k_half, k_half))

    tm_y = {d: (y + d) % n_y for d in range(n_y)}
    tm_x = {d: (x + d) % n_x for d in range(n_x)}
    tm_to = {(dy, dx): tm_y[dy] * n_x + tm_x[dx] for dy in range(n_y) for dx in range(n_x)}
    z_to = {d: (z + d) % n_z for d in range(n_z)}
    z_group = {d: (z // 2 + d) % n_g for d in range(n_g)}
    tm_order = sorted((o for o in tm_to if o != (0, 0)), key=lambda o: -min(o[0], n_y - o[0]) - min(o[1], n_x - o[1]))
    z_order = [d for d in far_first(n_z) if d]

    def remote(src, dst, send, recv, to_s, to_t):
        return pltpu.make_async_remote_copy(
            src_ref=src, dst_ref=dst, send_sem=send, recv_sem=recv, device_id=(to_s, to_t), device_id_type=MESH
        )

    def settle(ref, sem):
        pltpu.make_async_copy(ref, ref, sem).wait()

    barrier = pltpu.get_barrier_semaphore()
    greeted = [(s, tm_to[o]) for o in tm_order] + [(2 * z_to[d] + core, t) for d in z_order] + [(other, t)]
    for device in greeted:
        pl.semaphore_signal(barrier, inc=1, device_id=device, device_id_type=MESH)

    block_rows = n_x * LANES

    def tm_block(dy):
        return pl.ds(pl.multiple_of(tm_y[dy] * block_rows, block_rows), block_rows)

    sketch_copy = pltpu.make_async_copy(sketch_hbm, sketch, s_sem)
    sketch_copy.start()
    a_copies = {dy: pltpu.make_async_copy(a_hbm.at[tm_block(dy), :], a.at[tm_block(dy), :], a_sem.at[dy]) for dy in range(n_y)}
    for dy in far_first(n_y):
        a_copies[dy].start()

    def split(v, h, lanes):
        for term in range(3):
            low = v.astype(BF16)
            lhs[pl.ds((3 * h + term) * k_half, k_half), lanes] = low
            v = v - low.astype(F32)

    def terms(*hs):
        return lhs[pl.ds(3 * hs[0] * k_half, 3 * len(hs) * k_half), :]

    def join(acc):
        return acc[:k_half] + (acc[k_half : 2 * k_half] + acc[2 * k_half : 3 * k_half])

    def tm_multiply(stage, hs, dy):
        if stage == 0:
            acc = lax.dot_general(terms(*hs), a[tm_block(dy), :], NT, preferred_element_type=F32)
        else:
            acc = lax.dot_general(terms(*hs), a_turned[:, tm_block(dy)], NN, preferred_element_type=F32)
        for h in hs:
            val = join(acc[3 * (h - hs[0]) * k_half :])
            for e in range(n_x):
                tm_part[stage, tm_y[dy] * n_x + e, halves[h], :] = val[:, e * LANES : (e + 1) * LANES]

    def tm_send(stage, h, dy):
        for dx in far_first(n_x):
            if (dy, dx) != (0, 0):
                to = tm_to[dy, dx]
                remote(
                    tm_part.at[stage, to, halves[h], :], tm_in.at[stage, t, halves[h], :],
                    tm_rs_s.at[stage, h], tm_rs_r.at[stage, h], s, to,
                ).start()

    def tm_product(stage, h, between=None):
        for i, dy in enumerate(far_first(n_y)):
            tm_multiply(stage, (h,), dy)
            tm_send(stage, h, dy)
            if between and i == min(between[0], n_y - 1):
                between[1]()

    def tm_sum(stage, h):
        settle(tm_in.at[stage, pl.ds(0, n_t - 1), halves[h], :], tm_rs_r.at[stage, h])
        tm_in[stage, t, halves[h], :] = tm_part[stage, t, halves[h], :]
        total = tm_in[stage, 0, halves[h], :]
        for i in range(1, n_t):
            total = total + tm_in[stage, i, halves[h], :]
        return total

    def tm_gather(stage, h, chunk):
        tm_full[stage, t, halves[h], :] = chunk
        mine = tm_full.at[stage, t, halves[h], :]
        for o in tm_order:
            remote(mine, mine, tm_ag_s.at[stage, h], tm_ag_r.at[stage, h], s, tm_to[o]).start()

    def tm_take(stage, h, flat):
        settle(tm_full.at[stage, pl.ds(0, n_t - 1), halves[h], :], tm_ag_r.at[stage, h])
        for c in range(n_t):
            lanes = pl.ds(c * LANES, LANES)
            v = tm_full[stage, c, halves[h], :]
            flat[halves[h], lanes] = v
            split(v, h, lanes)

    def z_pair(dg):
        return pl.ds(2 * z_group[dg], 2)

    def sibling(stage, h, dg):
        return remote(
            z_part.at[stage, 1 - core, z_pair(dg), halves[h], :], sib_in.at[stage, z_pair(dg), halves[h], :],
            sib_s.at[stage, h, dg], sib_r.at[stage, h, dg], other, t,
        )

    def z_both(stage, h, dg):
        sibling(stage, h, dg).wait_recv()
        pair = z_pair(dg)
        z_send[stage, pair, halves[h], :] = z_part[stage, core, pair, halves[h], :] + sib_in[stage, pair, halves[h], :]
        tos = [2 * z_group[dg] + e for e in range(2)] if dg else [4 * (z // 2) + 1 - z]
        for to in tos:
            remote(
                z_send.at[stage, to, halves[h], :], z_in.at[stage, z, halves[h], :],
                z_rs_s.at[stage, h], z_rs_r.at[stage, h], 2 * to + core, t,
            ).start()

    def z_product(stage, h, between=None):
        before = None
        for i, dg in enumerate(far_first(n_g)):
            block = pl.ds(pl.multiple_of(z_group[dg] * 4 * LANES, 4 * LANES), 4 * LANES)
            acc = lax.dot_general(terms(h), a[:, block], NN, preferred_element_type=F32)
            val = join(acc)
            for e in range(4):
                z_part[stage, e % 2, 2 * z_group[dg] + e // 2, halves[h], :] = val[:, e * LANES : (e + 1) * LANES]
            sibling(stage, h, dg).start()
            if before is not None:
                z_both(stage, h, before)
            before = dg
            if between and i == min(between[0], n_g - 1):
                between[1]()

    def z_sum(stage, h):
        settle(z_in.at[stage, pl.ds(0, n_z - 1), halves[h], :], z_rs_r.at[stage, h])
        z_in[stage, z, halves[h], :] = z_send[stage, z, halves[h], :]
        total = z_in[stage, 0, halves[h], :]
        for i in range(1, n_z):
            total = total + z_in[stage, i, halves[h], :]
        return total

    def z_gather(stage, h, chunk):
        z_full[stage, core, z, halves[h], :] = chunk
        mine = z_full.at[stage, core, z, halves[h], :]
        for d in z_order:
            remote(mine, mine, z_ag_s.at[stage, h], z_ag_r.at[stage, h], 2 * z_to[d] + core, t).start()

    def z_forward(stage, h):
        settle(z_full.at[stage, core, pl.ds(0, n_z - 1), halves[h], :], z_ag_r.at[stage, h])
        mine = z_full.at[stage, core, :, halves[h], :]
        remote(mine, mine, fw_s.at[stage, h], fw_r.at[stage, h], other, t).start()

    def z_take(stage, h, flat, again=True):
        settle(z_full.at[stage, core, :, halves[h], :], fw_r.at[stage, h])
        for c in range(n_s):
            lanes = pl.ds(c * LANES, LANES)
            v = z_full[stage, c % 2, c // 2, halves[h], :]
            flat[halves[h], lanes] = v
            if again:
                split(v, h, lanes)

    def pack(flat, out):
        gram = exact(flat[...], flat[...], NT)
        for c in range(2):
            out[c, :, :k_all] = gram[c * k_quarter : (c + 1) * k_quarter]
            out[c, :, k_all:] = gram[k_half + c * k_quarter : k_half + (c + 1) * k_quarter]

    def gram_swap(i, total):
        g_sum[i, core] = total
        mine = g_sum.at[i, core]
        remote(mine, mine, gs_s.at[i], gs_r.at[i], other, t).start()

    def gram_end(i):
        settle(g_sum.at[i, core], gs_r.at[i])
        return g_sum[i]

    def gram_z_send(i, flat):
        pack(flat, g_out.at[i])
        remote(g_out.at[i, 1 - core], g_pair.at[i // 2], gp_s.at[i // 2], gp_r.at[i // 2], other, t).start()

    def gram_z_pair(i):
        b = i // 2
        settle(g_pair.at[b], gp_r.at[b])
        g_z[b, z] = g_out[i, core] + g_pair[b]
        mine = g_z.at[b, z]
        for d in z_order:
            remote(mine, mine, g_s.at[i], g_r.at[i], 2 * z_to[d] + core, t).start()

    def gram_z_middle(i):
        b = i // 2
        settle(g_z.at[b, pl.ds(0, n_z - 1)], g_r.at[i])
        total = g_z[b, 0]
        for k in range(1, n_z):
            total = total + g_z[b, k]
        gram_swap(i, total)

    def gram_tm_send(i, flat):
        pack(flat, g_out.at[i])
        g_tm[t] = g_out[i, core]
        mine = g_tm.at[t]
        for o in tm_order:
            remote(mine, mine, g_s.at[i], g_r.at[i], s, tm_to[o]).start()

    def gram_tm_middle(i):
        settle(g_tm.at[pl.ds(0, n_t - 1)], g_r.at[i])
        total = g_tm[0]
        for k in range(1, n_t):
            total = total + g_tm[k]
        gram_swap(i, total)

    def invert(i, packed):
        lane = lax.broadcasted_iota(jnp.int32, (k_all, 2 * k_all), 1)
        row = lax.broadcasted_iota(jnp.int32, (k_all, 2 * k_all), 0)
        work[...] = jnp.where(lane == row + k_all, 1.0, 0.0).astype(F32)
        for c in range(2):
            work[pl.ds(c * k_quarter, k_quarter), :k_all] = packed[c, :, :k_all]
            work[pl.ds(k_half + c * k_quarter, k_quarter), :k_all] = packed[c, :, k_all:]
        v = work[...]
        for j in range(0, k_all, PANEL):
            below = lax.broadcasted_iota(jnp.int32, v.shape, 0)
            col = [jnp.broadcast_to(v[:, j + m : j + m + 1], v.shape) for m in range(PANEL)]
            line = [v[m : m + 1, :] for m in range(PANEL)]
            for m in range(PANEL):
                factor = jnp.where(below > m, col[m] * (1.0 / col[m][m : m + 1, :]), 0.0)
                for n in range(m + 1, PANEL):
                    line[n] = line[n] - factor[n : n + 1, :] * line[m]
                    col[n] = col[n] - factor * col[n][m : m + 1, :]
                v = v - factor * line[m]
            done, v = v[:PANEL], v[PANEL:]
            mine = (lane == row + j)[:PANEL]
            diag = jnp.sum(jnp.where(mine, done, 0.0), axis=1, keepdims=True)
            invs[i, j : j + PANEL, :] = (done * lax.rsqrt(diag))[:, k_all:]

    def apply_a(i, low):
        return exact(invs[i, :k_half, :k_half], low)

    def apply_b(i, low, high):
        return exact(invs[i, k_half:, :k_half], low) + exact(invs[i, k_half:, k_half:], high)

    sketch_copy.wait()
    for h in range(2):
        split(sketch[halves[h], :], h, slice(None))

    for dy in far_first(n_y):
        a_copies[dy].wait()
        tm_multiply(0, (0, 1), dy)
    pl.semaphore_wait(barrier, len(greeted))
    for h in range(2):
        for dy in far_first(n_y):
            tm_send(0, h, dy)

    def turn(i, carry):
        block = pl.ds(pl.multiple_of(i * 2 * LANES, 2 * LANES), 2 * LANES)
        a_turned[:, block] = a[block, :].T
        return carry

    lax.fori_loop(0, rows // (2 * LANES), turn, 0)
    for h in range(2):
        tm_gather(0, h, tm_sum(0, h))
    tm_take(0, 0, flats.at[0])

    z_product(0, 0)
    tm_take(0, 1, flats.at[0])
    gram_z_send(0, flats.at[0])
    z_both(0, 0, 0)
    z_product(0, 1, (0, lambda: gram_z_pair(0)))
    z_both(0, 1, 0)
    z_gather(0, 0, z_sum(0, 0))
    gram_z_middle(0)
    z_gather(0, 1, z_sum(0, 1))
    invert(0, gram_end(0))
    z_forward(0, 0)
    z_take(0, 0, flats.at[1])

    tm_product(1, 0, (2, lambda: z_forward(0, 1)))
    z_take(0, 1, flats.at[1])
    tm_product(1, 1)
    tm_low[...] = tm_sum(1, 0)
    tm_gather(1, 0, apply_a(0, tm_low[...]))
    back_flat[...] = exact(invs[0], flats[1])
    gram_tm_send(1, back_flat)
    first_out[...] = (rows_total**0.5) * exact(invs[0], flats[0])
    tm_gather(1, 1, apply_b(0, tm_low[...], tm_sum(1, 1)))
    tm_take(1, 0, flats.at[2])

    z_product(1, 0, (1, lambda: gram_tm_middle(1)))
    z_both(1, 0, 0)
    invert(1, gram_end(1))
    tm_take(1, 1, flats.at[2])
    z_product(1, 1)
    z_both(1, 1, 0)
    z_low[...] = z_sum(1, 0)
    z_gather(1, 0, apply_a(1, z_low[...]))
    basis_flat[...] = exact(invs[1], flats[2])
    gram_z_send(2, basis_flat)
    gram_z_pair(2)
    z_gather(1, 1, apply_b(1, z_low[...], z_sum(1, 1)))
    back_out[...] = (cols_total**0.5) * exact(invs[1], back_flat[...])
    z_forward(1, 0)
    gram_z_middle(2)
    invert(2, gram_end(2))
    z_forward(1, 1)
    basis_out[...] = (rows_total**0.5) * exact(invs[2], basis_flat[...])
    z_take(1, 0, flats.at[3], again=False)
    proj_out[:k_half, :] = exact(invs[2, :k_half, :k_half], flats[3, :k_half, :])
    z_take(1, 1, flats.at[3], again=False)
    proj_out[k_half:, :] = exact(invs[2, k_half:, :], flats[3])

    for stage in range(2):
        for h in range(2):
            settle(tm_in.at[stage, pl.ds(0, n_t - 1), halves[h], :], tm_rs_s.at[stage, h])
            settle(z_in.at[stage, pl.ds(0, n_z - 1), halves[h], :], z_rs_s.at[stage, h])
            settle(tm_full.at[stage, pl.ds(0, n_t - 1), halves[h], :], tm_ag_s.at[stage, h])
            settle(z_full.at[stage, core, pl.ds(0, n_z - 1), halves[h], :], z_ag_s.at[stage, h])
            settle(z_full.at[stage, core, :, halves[h], :], fw_s.at[stage, h])
            for dg in range(n_g):
                settle(sib_in.at[stage, pl.ds(0, 2), halves[h], :], sib_s.at[stage, h, dg])
        settle(g_z.at[stage, pl.ds(0, n_z - 1)], g_s.at[2 * stage])
        settle(g_pair.at[stage], gp_s.at[stage])
    settle(g_tm.at[pl.ds(0, n_t - 1)], g_s.at[1])
    for i in range(3):
        settle(g_sum.at[i, core], gs_s.at[i])


def finish(*refs):
    sems = refs[-1]
    copies = [pltpu.make_async_copy(refs[i], refs[4 + i], sems.at[i]) for i in range(4)]
    for copy in copies:
        copy.start()
    for copy in copies:
        copy.wait()


def solution(mesh):
    n_s, n_t = mesh.shape["series"], mesh.shape["tm"]
    n_z, n_g = n_s // 2, n_s // 4

    def local(traffic, sketch):
        rows, cols = traffic.shape
        k = sketch.shape[1]
        vmem, hbm, anywhere = (pl.BlockSpec(memory_space=m) for m in (pltpu.VMEM, pltpu.HBM, pl.ANY))
        sem = pltpu.SemaphoreType.DMA
        chunk = (k, LANES)
        gram = (k // 4, 2 * k)
        by_rows, by_cols = jax.ShapeDtypeStruct((k, rows), F32), jax.ShapeDtypeStruct((k, cols), F32)
        outs = pl.pallas_call(
            functools.partial(kernel, n_s, n_t),
            out_shape=(by_rows, by_cols, by_rows, by_cols),
            in_specs=[hbm, hbm],
            out_specs=(vmem,) * 4,
            scratch_shapes=[
                pltpu.VMEM((rows, cols), BF16),
                pltpu.VMEM((cols, rows), BF16),
                pltpu.VMEM((k, cols), F32),
                pltpu.VMEM((3 * k, cols), BF16),
                pltpu.VMEM((2, n_t, *chunk), F32),
                pltpu.VMEM((2, n_t, *chunk), F32),
                pltpu.VMEM((2, n_t, *chunk), F32),
                pltpu.VMEM((2, 2, n_z, *chunk), F32),
                pltpu.VMEM((2, n_z, *chunk), F32),
                pltpu.VMEM((2, n_z, *chunk), F32),
                pltpu.VMEM((2, n_z, *chunk), F32),
                pltpu.VMEM((2, 2, n_z, *chunk), F32),
                pltpu.VMEM((4, k, cols), F32),
                pltpu.VMEM((k, cols), F32),
                pltpu.VMEM((k, rows), F32),
                pltpu.VMEM((k // 2, LANES), F32),
                pltpu.VMEM((k // 2, LANES), F32),
                pltpu.VMEM((3, k, k), F32),
                pltpu.VMEM((k, 2 * k), F32),
                pltpu.VMEM((3, 2, *gram), F32),
                pltpu.VMEM((2, *gram), F32),
                pltpu.VMEM((n_t, *gram), F32),
                pltpu.VMEM((2, n_z, *gram), F32),
                pltpu.VMEM((3, 2, *gram), F32),
                sem((math.isqrt(n_t),)), sem,
                sem((2, 2)), sem((2, 2)), sem((2, 2)), sem((2, 2)),
                sem((2, 2, n_g)), sem((2, 2, n_g)),
                sem((2, 2)), sem((2, 2)), sem((2, 2)), sem((2, 2)), sem((2, 2)), sem((2, 2)),
                sem((2,)), sem((2,)), sem((3,)), sem((3,)), sem((3,)), sem((3,)),
            ],
            compiler_params=pltpu.CompilerParams(
                collective_id=0, has_side_effects=True, vmem_limit_bytes=48 * 2**20
            ),
            name="range_finder",
        )(traffic, pltpu.with_memory_space_constraint(sketch.T, pltpu.HBM))
        first, back, basis, proj = pl.pallas_call(
            finish,
            out_shape=(by_rows, by_cols, by_rows, by_cols),
            in_specs=[anywhere] * 4,
            out_specs=(anywhere,) * 4,
            scratch_shapes=[sem((4,))],
            compiler_params=pltpu.CompilerParams(vmem_limit_bytes=8 * 2**20),
            name="finish",
        )(*outs)
        return first.T, back.T, basis.T, proj

    in_specs = (P("series", "tm"), P("tm", None))
    out_specs = (P("series", None), P("tm", None), P("series", None), P(None, "tm"))
    return jax.shard_map(local, mesh=mesh, in_specs=in_specs, out_specs=out_specs, check_vma=False)
```

```python
import functools
import math

import jax
import jax.numpy as jnp
from jax import lax
from jax.experimental import pallas as pl
from jax.experimental.pallas import tpu as pltpu
from jax.sharding import PartitionSpec as P

F32, BF16 = jnp.float32, jnp.bfloat16
HIGHEST = lax.Precision.HIGHEST
MESH = pl.DeviceIdType.MESH
LANES = 128
PANEL = 16
NN = (((1,), (0,)), ((), ()))
NT = (((1,), (1,)), ((), ()))


def far_first(n):
    return sorted(range(n), key=lambda d: (-min(d, n - d), d))


def exact(x, y, dims=NN):
    return lax.dot_general(x, y, dims, precision=HIGHEST, preferred_element_type=F32)


def kernel(
    n_s, n_t, a_hbm, sketch_hbm, first_out, back_out, basis_out, proj_out,
    a, a_turned, sketch, lhs, tm_part, tm_in, tm_full, z_part, sib_in, z_send, z_in, z_full, flats, back_flat, basis_flat, tm_low, z_low, invs, work,
    g_out, g_pair, g_tm, g_z, g_sum,
    a_sem, s_sem, tm_rs_s, tm_rs_r, tm_ag_s, tm_ag_r, sib_s, sib_r, z_rs_s, z_rs_r, z_ag_s, z_ag_r, fw_s, fw_r,
    gp_s, gp_r, g_s, g_r, gs_s, gs_r,
):
    n_z, n_g = n_s // 2, n_s // 4
    n_x = math.isqrt(n_t)
    n_y = n_t // n_x
    k_all = sketch.shape[0]
    k_half, k_quarter = k_all // 2, k_all // 4
    rows, cols = a.shape
    rows_total, cols_total = rows * n_s, cols * n_t
    s, t = lax.axis_index("series"), lax.axis_index("tm")
    z, core, y, x = s // 2, s % 2, t // n_x, t % n_x
    other = 2 * z + 1 - core
    halves = (pl.ds(0, k_half), pl.ds(k_half, k_half))

    tm_y = {d: (y + d) % n_y for d in range(n_y)}
    tm_x = {d: (x + d) % n_x for d in range(n_x)}
    tm_to = {(dy, dx): tm_y[dy] * n_x + tm_x[dx] for dy in range(n_y) for dx in range(n_x)}
    z_to = {d: (z + d) % n_z for d in range(n_z)}
    z_group = {d: (z // 2 + d) % n_g for d in range(n_g)}
    tm_order = sorted((o for o in tm_to if o != (0, 0)), key=lambda o: -min(o[0], n_y - o[0]) - min(o[1], n_x - o[1]))
    z_order = [d for d in far_first(n_z) if d]

    def remote(src, dst, send, recv, to_s, to_t):
        return pltpu.make_async_remote_copy(
            src_ref=src, dst_ref=dst, send_sem=send, recv_sem=recv, device_id=(to_s, to_t), device_id_type=MESH
        )

    def settle(ref, sem):
        pltpu.make_async_copy(ref, ref, sem).wait()

    barrier = pltpu.get_barrier_semaphore()
    greeted = [(s, tm_to[o]) for o in tm_order] + [(2 * z_to[d] + core, t) for d in z_order] + [(other, t)]
    for device in greeted:
        pl.semaphore_signal(barrier, inc=1, device_id=device, device_id_type=MESH)

    block_rows = n_x * LANES

    def tm_block(dy):
        return pl.ds(pl.multiple_of(tm_y[dy] * block_rows, block_rows), block_rows)

    sketch_copy = pltpu.make_async_copy(sketch_hbm, sketch, s_sem)
    sketch_copy.start()
    a_copies = {dy: pltpu.make_async_copy(a_hbm.at[tm_block(dy), :], a.at[tm_block(dy), :], a_sem.at[dy]) for dy in range(n_y)}
    for dy in far_first(n_y):
        a_copies[dy].start()

    def split(v, h, lanes):
        for term in range(3):
            low = v.astype(BF16)
            lhs[pl.ds((3 * h + term) * k_half, k_half), lanes] = low
            v = v - low.astype(F32)

    def terms(*hs):
        return lhs[pl.ds(3 * hs[0] * k_half, 3 * len(hs) * k_half), :]

    def join(acc):
        return acc[:k_half] + (acc[k_half : 2 * k_half] + acc[2 * k_half : 3 * k_half])

    def tm_multiply(stage, hs, dy):
        if stage == 0:
            acc = lax.dot_general(terms(*hs), a[tm_block(dy), :], NT, preferred_element_type=F32)
        else:
            acc = lax.dot_general(terms(*hs), a_turned[:, tm_block(dy)], NN, preferred_element_type=F32)
        for h in hs:
            val = join(acc[3 * (h - hs[0]) * k_half :])
            for e in range(n_x):
                tm_part[stage, tm_y[dy] * n_x + e, halves[h], :] = val[:, e * LANES : (e + 1) * LANES]

    def tm_send(stage, h, dy):
        for dx in far_first(n_x):
            if (dy, dx) != (0, 0):
                to = tm_to[dy, dx]
                remote(
                    tm_part.at[stage, to, halves[h], :], tm_in.at[stage, t, halves[h], :],
                    tm_rs_s.at[stage, h], tm_rs_r.at[stage, h], s, to,
                ).start()

    def tm_product(stage, h, between=None):
        for i, dy in enumerate(far_first(n_y)):
            tm_multiply(stage, (h,), dy)
            tm_send(stage, h, dy)
            if between and i == min(between[0], n_y - 1):
                between[1]()

    def tm_sum(stage, h):
        settle(tm_in.at[stage, pl.ds(0, n_t - 1), halves[h], :], tm_rs_r.at[stage, h])
        tm_in[stage, t, halves[h], :] = tm_part[stage, t, halves[h], :]
        total = tm_in[stage, 0, halves[h], :]
        for i in range(1, n_t):
            total = total + tm_in[stage, i, halves[h], :]
        return total

    def tm_gather(stage, h, chunk):
        tm_full[stage, t, halves[h], :] = chunk
        mine = tm_full.at[stage, t, halves[h], :]
        for o in tm_order:
            remote(mine, mine, tm_ag_s.at[stage, h], tm_ag_r.at[stage, h], s, tm_to[o]).start()

    def tm_take(stage, h, flat):
        settle(tm_full.at[stage, pl.ds(0, n_t - 1), halves[h], :], tm_ag_r.at[stage, h])
        for c in range(n_t):
            lanes = pl.ds(c * LANES, LANES)
            v = tm_full[stage, c, halves[h], :]
            flat[halves[h], lanes] = v
            split(v, h, lanes)

    def z_pair(dg):
        return pl.ds(2 * z_group[dg], 2)

    def sibling(stage, h, dg):
        return remote(
            z_part.at[stage, 1 - core, z_pair(dg), halves[h], :], sib_in.at[stage, z_pair(dg), halves[h], :],
            sib_s.at[stage, h, dg], sib_r.at[stage, h, dg], other, t,
        )

    def z_both(stage, h, dg):
        sibling(stage, h, dg).wait_recv()
        pair = z_pair(dg)
        z_send[stage, pair, halves[h], :] = z_part[stage, core, pair, halves[h], :] + sib_in[stage, pair, halves[h], :]
        tos = [2 * z_group[dg] + e for e in range(2)] if dg else [4 * (z // 2) + 1 - z]
        for to in tos:
            remote(
                z_send.at[stage, to, halves[h], :], z_in.at[stage, z, halves[h], :],
                z_rs_s.at[stage, h], z_rs_r.at[stage, h], 2 * to + core, t,
            ).start()

    def z_product(stage, h, between=None):
        before = None
        for i, dg in enumerate(far_first(n_g)):
            block = pl.ds(pl.multiple_of(z_group[dg] * 4 * LANES, 4 * LANES), 4 * LANES)
            acc = lax.dot_general(terms(h), a[:, block], NN, preferred_element_type=F32)
            val = join(acc)
            for e in range(4):
                z_part[stage, e % 2, 2 * z_group[dg] + e // 2, halves[h], :] = val[:, e * LANES : (e + 1) * LANES]
            sibling(stage, h, dg).start()
            if before is not None:
                z_both(stage, h, before)
            before = dg
            if between and i == min(between[0], n_g - 1):
                between[1]()

    def z_sum(stage, h):
        settle(z_in.at[stage, pl.ds(0, n_z - 1), halves[h], :], z_rs_r.at[stage, h])
        z_in[stage, z, halves[h], :] = z_send[stage, z, halves[h], :]
        total = z_in[stage, 0, halves[h], :]
        for i in range(1, n_z):
            total = total + z_in[stage, i, halves[h], :]
        return total

    def z_gather(stage, h, chunk):
        z_full[stage, core, z, halves[h], :] = chunk
        mine = z_full.at[stage, core, z, halves[h], :]
        for d in z_order:
            remote(mine, mine, z_ag_s.at[stage, h], z_ag_r.at[stage, h], 2 * z_to[d] + core, t).start()

    def z_forward(stage, h):
        settle(z_full.at[stage, core, pl.ds(0, n_z - 1), halves[h], :], z_ag_r.at[stage, h])
        mine = z_full.at[stage, core, :, halves[h], :]
        remote(mine, mine, fw_s.at[stage, h], fw_r.at[stage, h], other, t).start()

    def z_take(stage, h, flat, again=True):
        settle(z_full.at[stage, core, :, halves[h], :], fw_r.at[stage, h])
        for c in range(n_s):
            lanes = pl.ds(c * LANES, LANES)
            v = z_full[stage, c % 2, c // 2, halves[h], :]
            flat[halves[h], lanes] = v
            if again:
                split(v, h, lanes)

    def pack(flat, out):
        gram = exact(flat[...], flat[...], NT)
        for c in range(2):
            out[c, :, :k_all] = gram[c * k_quarter : (c + 1) * k_quarter]
            out[c, :, k_all:] = gram[k_half + c * k_quarter : k_half + (c + 1) * k_quarter]

    def gram_swap(i, total):
        g_sum[i, core] = total
        mine = g_sum.at[i, core]
        remote(mine, mine, gs_s.at[i], gs_r.at[i], other, t).start()

    def gram_end(i):
        settle(g_sum.at[i, core], gs_r.at[i])
        return g_sum[i]

    def gram_z_send(i, flat):
        pack(flat, g_out.at[i])
        remote(g_out.at[i, 1 - core], g_pair.at[i // 2], gp_s.at[i // 2], gp_r.at[i // 2], other, t).start()

    def gram_z_pair(i):
        b = i // 2
        settle(g_pair.at[b], gp_r.at[b])
        g_z[b, z] = g_out[i, core] + g_pair[b]
        mine = g_z.at[b, z]
        for d in z_order:
            remote(mine, mine, g_s.at[i], g_r.at[i], 2 * z_to[d] + core, t).start()

    def gram_z_middle(i):
        b = i // 2
        settle(g_z.at[b, pl.ds(0, n_z - 1)], g_r.at[i])
        total = g_z[b, 0]
        for k in range(1, n_z):
            total = total + g_z[b, k]
        gram_swap(i, total)

    def gram_tm_send(i, flat):
        pack(flat, g_out.at[i])
        g_tm[t] = g_out[i, core]
        mine = g_tm.at[t]
        for o in tm_order:
            remote(mine, mine, g_s.at[i], g_r.at[i], s, tm_to[o]).start()

    def gram_tm_middle(i):
        settle(g_tm.at[pl.ds(0, n_t - 1)], g_r.at[i])
        total = g_tm[0]
        for k in range(1, n_t):
            total = total + g_tm[k]
        gram_swap(i, total)

    def invert(i, packed):
        lane = lax.broadcasted_iota(jnp.int32, (k_all, 2 * k_all), 1)
        row = lax.broadcasted_iota(jnp.int32, (k_all, 2 * k_all), 0)
        work[...] = jnp.where(lane == row + k_all, 1.0, 0.0).astype(F32)
        for c in range(2):
            work[pl.ds(c * k_quarter, k_quarter), :k_all] = packed[c, :, :k_all]
            work[pl.ds(k_half + c * k_quarter, k_quarter), :k_all] = packed[c, :, k_all:]
        v = work[...]
        for j in range(0, k_all, PANEL):
            below = lax.broadcasted_iota(jnp.int32, v.shape, 0)
            col = [jnp.broadcast_to(v[:, j + m : j + m + 1], v.shape) for m in range(PANEL)]
            line = [v[m : m + 1, :] for m in range(PANEL)]
            for m in range(PANEL):
                factor = jnp.where(below > m, col[m], 0.0) * (1.0 / col[m][m : m + 1, :])
                for n in range(m + 1, PANEL):
                    line[n] = line[n] - factor[n : n + 1, :] * line[m]
                    col[n] = col[n] - factor * col[n][m : m + 1, :]
                v = v - factor * line[m]
            done, v = v[:PANEL], v[PANEL:]
            mine = (lane == row + j)[:PANEL]
            diag = jnp.sum(jnp.where(mine, done, 0.0), axis=1, keepdims=True)
            invs[i, j : j + PANEL, :] = (done * lax.rsqrt(diag))[:, k_all:]

    def apply_a(i, low):
        return exact(invs[i, :k_half, :k_half], low)

    def apply_b(i, low, high):
        return exact(invs[i, k_half:, :k_half], low) + exact(invs[i, k_half:, k_half:], high)

    sketch_copy.wait()
    for h in range(2):
        split(sketch[halves[h], :], h, slice(None))

    for dy in far_first(n_y):
        a_copies[dy].wait()
        tm_multiply(0, (0, 1), dy)
    pl.semaphore_wait(barrier, len(greeted))
    for h in range(2):
        for dy in far_first(n_y):
            tm_send(0, h, dy)

    def turn(i, carry):
        block = pl.ds(pl.multiple_of(i * 2 * LANES, 2 * LANES), 2 * LANES)
        a_turned[:, block] = a[block, :].T
        return carry

    lax.fori_loop(0, rows // (2 * LANES), turn, 0)
    for h in range(2):
        tm_gather(0, h, tm_sum(0, h))
    tm_take(0, 0, flats.at[0])

    z_product(0, 0)
    tm_take(0, 1, flats.at[0])
    gram_z_send(0, flats.at[0])
    z_both(0, 0, 0)
    z_product(0, 1, (0, lambda: gram_z_pair(0)))
    z_both(0, 1, 0)
    z_gather(0, 0, z_sum(0, 0))
    gram_z_middle(0)
    z_gather(0, 1, z_sum(0, 1))
    invert(0, gram_end(0))
    z_forward(0, 0)
    z_take(0, 0, flats.at[1])

    tm_product(1, 0, (2, lambda: z_forward(0, 1)))
    z_take(0, 1, flats.at[1])
    tm_product(1, 1)
    tm_low[...] = tm_sum(1, 0)
    tm_gather(1, 0, apply_a(0, tm_low[...]))
    back_flat[...] = exact(invs[0], flats[1])
    gram_tm_send(1, back_flat)
    first_out[...] = (rows_total**0.5) * exact(invs[0], flats[0])
    tm_gather(1, 1, apply_b(0, tm_low[...], tm_sum(1, 1)))
    tm_take(1, 0, flats.at[2])

    z_product(1, 0, (1, lambda: gram_tm_middle(1)))
    packed = gram_end(1)
    z_both(1, 0, 0)
    invert(1, packed)
    tm_take(1, 1, flats.at[2])
    z_product(1, 1)
    z_both(1, 1, 0)
    z_low[...] = z_sum(1, 0)
    z_gather(1, 0, apply_a(1, z_low[...]))
    basis_flat[...] = exact(invs[1], flats[2])
    gram_z_send(2, basis_flat)
    gram_z_pair(2)
    z_gather(1, 1, apply_b(1, z_low[...], z_sum(1, 1)))
    back_out[...] = (cols_total**0.5) * exact(invs[1], back_flat[...])
    z_forward(1, 0)
    gram_z_middle(2)
    invert(2, gram_end(2))
    z_forward(1, 1)
    basis_out[...] = (rows_total**0.5) * exact(invs[2], basis_flat[...])
    z_take(1, 0, flats.at[3], again=False)
    proj_out[:k_half, :] = exact(invs[2, :k_half, :k_half], flats[3, :k_half, :])
    z_take(1, 1, flats.at[3], again=False)
    proj_out[k_half:, :] = exact(invs[2, k_half:, :], flats[3])

    for stage in range(2):
        for h in range(2):
            settle(tm_in.at[stage, pl.ds(0, n_t - 1), halves[h], :], tm_rs_s.at[stage, h])
            settle(z_in.at[stage, pl.ds(0, n_z - 1), halves[h], :], z_rs_s.at[stage, h])
            settle(tm_full.at[stage, pl.ds(0, n_t - 1), halves[h], :], tm_ag_s.at[stage, h])
            settle(z_full.at[stage, core, pl.ds(0, n_z - 1), halves[h], :], z_ag_s.at[stage, h])
            settle(z_full.at[stage, core, :, halves[h], :], fw_s.at[stage, h])
            for dg in range(n_g):
                settle(sib_in.at[stage, pl.ds(0, 2), halves[h], :], sib_s.at[stage, h, dg])
        settle(g_z.at[stage, pl.ds(0, n_z - 1)], g_s.at[2 * stage])
        settle(g_pair.at[stage], gp_s.at[stage])
    settle(g_tm.at[pl.ds(0, n_t - 1)], g_s.at[1])
    for i in range(3):
        settle(g_sum.at[i, core], gs_s.at[i])


def finish(*refs):
    sems = refs[-1]
    copies = [pltpu.make_async_copy(refs[i], refs[4 + i], sems.at[i]) for i in range(4)]
    for copy in copies:
        copy.start()
    for copy in copies:
        copy.wait()


def solution(mesh):
    n_s, n_t = mesh.shape["series"], mesh.shape["tm"]
    n_z, n_g = n_s // 2, n_s // 4

    def local(traffic, sketch):
        rows, cols = traffic.shape
        k = sketch.shape[1]
        vmem, hbm, anywhere = (pl.BlockSpec(memory_space=m) for m in (pltpu.VMEM, pltpu.HBM, pl.ANY))
        sem = pltpu.SemaphoreType.DMA
        chunk = (k, LANES)
        gram = (k // 4, 2 * k)
        by_rows, by_cols = jax.ShapeDtypeStruct((k, rows), F32), jax.ShapeDtypeStruct((k, cols), F32)
        outs = pl.pallas_call(
            functools.partial(kernel, n_s, n_t),
            out_shape=(by_rows, by_cols, by_rows, by_cols),
            in_specs=[hbm, hbm],
            out_specs=(vmem,) * 4,
            scratch_shapes=[
                pltpu.VMEM((rows, cols), BF16),
                pltpu.VMEM((cols, rows), BF16),
                pltpu.VMEM((k, cols), F32),
                pltpu.VMEM((3 * k, cols), BF16),
                pltpu.VMEM((2, n_t, *chunk), F32),
                pltpu.VMEM((2, n_t, *chunk), F32),
                pltpu.VMEM((2, n_t, *chunk), F32),
                pltpu.VMEM((2, 2, n_z, *chunk), F32),
                pltpu.VMEM((2, n_z, *chunk), F32),
                pltpu.VMEM((2, n_z, *chunk), F32),
                pltpu.VMEM((2, n_z, *chunk), F32),
                pltpu.VMEM((2, 2, n_z, *chunk), F32),
                pltpu.VMEM((4, k, cols), F32),
                pltpu.VMEM((k, cols), F32),
                pltpu.VMEM((k, rows), F32),
                pltpu.VMEM((k // 2, LANES), F32),
                pltpu.VMEM((k // 2, LANES), F32),
                pltpu.VMEM((3, k, k), F32),
                pltpu.VMEM((k, 2 * k), F32),
                pltpu.VMEM((3, 2, *gram), F32),
                pltpu.VMEM((2, *gram), F32),
                pltpu.VMEM((n_t, *gram), F32),
                pltpu.VMEM((2, n_z, *gram), F32),
                pltpu.VMEM((3, 2, *gram), F32),
                sem((math.isqrt(n_t),)), sem,
                sem((2, 2)), sem((2, 2)), sem((2, 2)), sem((2, 2)),
                sem((2, 2, n_g)), sem((2, 2, n_g)),
                sem((2, 2)), sem((2, 2)), sem((2, 2)), sem((2, 2)), sem((2, 2)), sem((2, 2)),
                sem((2,)), sem((2,)), sem((3,)), sem((3,)), sem((3,)), sem((3,)),
            ],
            compiler_params=pltpu.CompilerParams(
                collective_id=0, has_side_effects=True, vmem_limit_bytes=48 * 2**20
            ),
            name="range_finder",
        )(traffic, pltpu.with_memory_space_constraint(sketch.T, pltpu.HBM))
        first, back, basis, proj = pl.pallas_call(
            finish,
            out_shape=(by_rows, by_cols, by_rows, by_cols),
            in_specs=[anywhere] * 4,
            out_specs=(anywhere,) * 4,
            scratch_shapes=[sem((4,))],
            compiler_params=pltpu.CompilerParams(vmem_limit_bytes=8 * 2**20),
            name="finish",
        )(*outs)
        return first.T, back.T, basis.T, proj

    in_specs = (P("series", "tm"), P("tm", None))
    out_specs = (P("series", None), P("tm", None), P("series", None), P(None, "tm"))
    return jax.shard_map(local, mesh=mesh, in_specs=in_specs, out_specs=out_specs, check_vma=False)
```

```python
import functools
import math

import jax
import jax.numpy as jnp
from jax import lax
from jax.experimental import pallas as pl
from jax.experimental.pallas import tpu as pltpu
from jax.sharding import PartitionSpec as P

F32, BF16 = jnp.float32, jnp.bfloat16
HIGHEST = lax.Precision.HIGHEST
MESH = pl.DeviceIdType.MESH
LANES = 128
PANEL = 16
NN = (((1,), (0,)), ((), ()))
NT = (((1,), (1,)), ((), ()))


def far_first(n):
    return sorted(range(n), key=lambda d: (-min(d, n - d), d))


def exact(x, y, dims=NN):
    return lax.dot_general(x, y, dims, precision=HIGHEST, preferred_element_type=F32)


def kernel(
    n_s, n_t, a_hbm, sketch_hbm, first_out, back_out, basis_out, proj_out,
    a, a_turned, sketch, lhs, tm_part, tm_in, tm_full, z_part, sib_in, z_send, z_in, z_full, flats, back_flat, basis_flat, tm_low, z_low, invs, work,
    g_out, g_pair, g_tm, g_z, g_sum,
    a_sem, s_sem, tm_rs_s, tm_rs_r, tm_ag_s, tm_ag_r, sib_s, sib_r, z_rs_s, z_rs_r, z_ag_s, z_ag_r, fw_s, fw_r,
    gp_s, gp_r, g_s, g_r, gs_s, gs_r,
):
    n_z, n_g = n_s // 2, n_s // 4
    n_x = math.isqrt(n_t)
    n_y = n_t // n_x
    k_all = sketch.shape[0]
    k_half, k_quarter = k_all // 2, k_all // 4
    rows, cols = a.shape
    rows_total, cols_total = rows * n_s, cols * n_t
    s, t = lax.axis_index("series"), lax.axis_index("tm")
    z, core, y, x = s // 2, s % 2, t // n_x, t % n_x
    other = 2 * z + 1 - core
    halves = (pl.ds(0, k_half), pl.ds(k_half, k_half))

    tm_y = {d: (y + d) % n_y for d in range(n_y)}
    tm_x = {d: (x + d) % n_x for d in range(n_x)}
    tm_to = {(dy, dx): tm_y[dy] * n_x + tm_x[dx] for dy in range(n_y) for dx in range(n_x)}
    z_to = {d: (z + d) % n_z for d in range(n_z)}
    z_group = {d: (z // 2 + d) % n_g for d in range(n_g)}
    tm_order = sorted((o for o in tm_to if o != (0, 0)), key=lambda o: -min(o[0], n_y - o[0]) - min(o[1], n_x - o[1]))
    z_order = [d for d in far_first(n_z) if d]

    def remote(src, dst, send, recv, to_s, to_t):
        return pltpu.make_async_remote_copy(
            src_ref=src, dst_ref=dst, send_sem=send, recv_sem=recv, device_id=(to_s, to_t), device_id_type=MESH
        )

    def settle(ref, sem):
        pltpu.make_async_copy(ref, ref, sem).wait()

    barrier = pltpu.get_barrier_semaphore()
    greeted = [(s, tm_to[o]) for o in tm_order] + [(2 * z_to[d] + core, t) for d in z_order] + [(other, t)]
    for device in greeted:
        pl.semaphore_signal(barrier, inc=1, device_id=device, device_id_type=MESH)

    block_rows = n_x * LANES

    def tm_block(dy):
        return pl.ds(pl.multiple_of(tm_y[dy] * block_rows, block_rows), block_rows)

    sketch_copy = pltpu.make_async_copy(sketch_hbm, sketch, s_sem)
    sketch_copy.start()
    a_copies = {dy: pltpu.make_async_copy(a_hbm.at[tm_block(dy), :], a.at[tm_block(dy), :], a_sem.at[dy]) for dy in range(n_y)}
    for dy in far_first(n_y):
        a_copies[dy].start()

    def split(v, h, lanes):
        for term in range(3):
            low = v.astype(BF16)
            lhs[pl.ds((3 * h + term) * k_half, k_half), lanes] = low
            v = v - low.astype(F32)

    def terms(*hs):
        return lhs[pl.ds(3 * hs[0] * k_half, 3 * len(hs) * k_half), :]

    def join(acc):
        return acc[:k_half] + (acc[k_half : 2 * k_half] + acc[2 * k_half : 3 * k_half])

    def tm_multiply(stage, hs, dy):
        if stage == 0:
            acc = lax.dot_general(terms(*hs), a[tm_block(dy), :], NT, preferred_element_type=F32)
        else:
            acc = lax.dot_general(terms(*hs), a_turned[:, tm_block(dy)], NN, preferred_element_type=F32)
        for h in hs:
            val = join(acc[3 * (h - hs[0]) * k_half :])
            for e in range(n_x):
                tm_part[stage, tm_y[dy] * n_x + e, halves[h], :] = val[:, e * LANES : (e + 1) * LANES]

    def tm_send(stage, h, dy):
        for dx in far_first(n_x):
            if (dy, dx) != (0, 0):
                to = tm_to[dy, dx]
                remote(
                    tm_part.at[stage, to, halves[h], :], tm_in.at[stage, t, halves[h], :],
                    tm_rs_s.at[stage, h], tm_rs_r.at[stage, h], s, to,
                ).start()

    def tm_product(stage, h, between=None):
        for i, dy in enumerate(far_first(n_y)):
            tm_multiply(stage, (h,), dy)
            tm_send(stage, h, dy)
            if between and i == min(between[0], n_y - 1):
                between[1]()

    def tm_sum(stage, h):
        settle(tm_in.at[stage, pl.ds(0, n_t - 1), halves[h], :], tm_rs_r.at[stage, h])
        tm_in[stage, t, halves[h], :] = tm_part[stage, t, halves[h], :]
        total = tm_in[stage, 0, halves[h], :]
        for i in range(1, n_t):
            total = total + tm_in[stage, i, halves[h], :]
        return total

    def tm_gather(stage, h, chunk):
        tm_full[stage, t, halves[h], :] = chunk
        mine = tm_full.at[stage, t, halves[h], :]
        for o in tm_order:
            remote(mine, mine, tm_ag_s.at[stage, h], tm_ag_r.at[stage, h], s, tm_to[o]).start()

    def tm_take(stage, h, flat):
        settle(tm_full.at[stage, pl.ds(0, n_t - 1), halves[h], :], tm_ag_r.at[stage, h])
        for c in range(n_t):
            lanes = pl.ds(c * LANES, LANES)
            v = tm_full[stage, c, halves[h], :]
            flat[halves[h], lanes] = v
            split(v, h, lanes)

    def z_pair(dg):
        return pl.ds(2 * z_group[dg], 2)

    def sibling(stage, h, dg):
        return remote(
            z_part.at[stage, 1 - core, z_pair(dg), halves[h], :], sib_in.at[stage, z_pair(dg), halves[h], :],
            sib_s.at[stage, h, dg], sib_r.at[stage, h, dg], other, t,
        )

    def z_both(stage, h, dg):
        sibling(stage, h, dg).wait_recv()
        pair = z_pair(dg)
        z_send[stage, pair, halves[h], :] = z_part[stage, core, pair, halves[h], :] + sib_in[stage, pair, halves[h], :]
        tos = [2 * z_group[dg] + e for e in range(2)] if dg else [4 * (z // 2) + 1 - z]
        for to in tos:
            remote(
                z_send.at[stage, to, halves[h], :], z_in.at[stage, z, halves[h], :],
                z_rs_s.at[stage, h], z_rs_r.at[stage, h], 2 * to + core, t,
            ).start()

    def z_product(stage, h, between=None):
        before = None
        for i, dg in enumerate(far_first(n_g)):
            block = pl.ds(pl.multiple_of(z_group[dg] * 4 * LANES, 4 * LANES), 4 * LANES)
            acc = lax.dot_general(terms(h), a[:, block], NN, preferred_element_type=F32)
            val = join(acc)
            for e in range(4):
                z_part[stage, e % 2, 2 * z_group[dg] + e // 2, halves[h], :] = val[:, e * LANES : (e + 1) * LANES]
            sibling(stage, h, dg).start()
            if before is not None:
                z_both(stage, h, before)
            before = dg
            if between and i == min(between[0], n_g - 1):
                between[1]()

    def z_sum(stage, h):
        settle(z_in.at[stage, pl.ds(0, n_z - 1), halves[h], :], z_rs_r.at[stage, h])
        z_in[stage, z, halves[h], :] = z_send[stage, z, halves[h], :]
        total = z_in[stage, 0, halves[h], :]
        for i in range(1, n_z):
            total = total + z_in[stage, i, halves[h], :]
        return total

    def z_gather(stage, h, chunk):
        z_full[stage, core, z, halves[h], :] = chunk
        mine = z_full.at[stage, core, z, halves[h], :]
        for d in z_order:
            remote(mine, mine, z_ag_s.at[stage, h], z_ag_r.at[stage, h], 2 * z_to[d] + core, t).start()

    def z_forward(stage, h):
        settle(z_full.at[stage, core, pl.ds(0, n_z - 1), halves[h], :], z_ag_r.at[stage, h])
        mine = z_full.at[stage, core, :, halves[h], :]
        remote(mine, mine, fw_s.at[stage, h], fw_r.at[stage, h], other, t).start()

    def z_take(stage, h, flat, again=True):
        settle(z_full.at[stage, core, :, halves[h], :], fw_r.at[stage, h])
        for c in range(n_s):
            lanes = pl.ds(c * LANES, LANES)
            v = z_full[stage, c % 2, c // 2, halves[h], :]
            flat[halves[h], lanes] = v
            if again:
                split(v, h, lanes)

    def pack(flat, out):
        gram = exact(flat[...], flat[...], NT)
        for c in range(2):
            out[c, :, :k_all] = gram[c * k_quarter : (c + 1) * k_quarter]
            out[c, :, k_all:] = gram[k_half + c * k_quarter : k_half + (c + 1) * k_quarter]

    def gram_swap(i, total):
        g_sum[i, core] = total
        mine = g_sum.at[i, core]
        remote(mine, mine, gs_s.at[i], gs_r.at[i], other, t).start()

    def gram_end(i):
        settle(g_sum.at[i, core], gs_r.at[i])
        return g_sum[i]

    def gram_z_send(i, flat):
        pack(flat, g_out.at[i])
        remote(g_out.at[i, 1 - core], g_pair.at[i // 2], gp_s.at[i // 2], gp_r.at[i // 2], other, t).start()

    def gram_z_pair(i):
        b = i // 2
        settle(g_pair.at[b], gp_r.at[b])
        g_z[b, z] = g_out[i, core] + g_pair[b]
        mine = g_z.at[b, z]
        for d in z_order:
            remote(mine, mine, g_s.at[i], g_r.at[i], 2 * z_to[d] + core, t).start()

    def gram_z_middle(i):
        b = i // 2
        settle(g_z.at[b, pl.ds(0, n_z - 1)], g_r.at[i])
        total = g_z[b, 0]
        for k in range(1, n_z):
            total = total + g_z[b, k]
        gram_swap(i, total)

    def gram_tm_send(i, flat):
        pack(flat, g_out.at[i])
        g_tm[t] = g_out[i, core]
        mine = g_tm.at[t]
        for o in tm_order:
            remote(mine, mine, g_s.at[i], g_r.at[i], s, tm_to[o]).start()

    def gram_tm_middle(i):
        settle(g_tm.at[pl.ds(0, n_t - 1)], g_r.at[i])
        total = g_tm[0]
        for k in range(1, n_t):
            total = total + g_tm[k]
        gram_swap(i, total)

    def invert(i, packed, start=0, stop=None):
        stop = k_all if stop is None else stop
        lane = lax.broadcasted_iota(jnp.int32, (k_all, 2 * k_all), 1)
        row = lax.broadcasted_iota(jnp.int32, (k_all, 2 * k_all), 0)
        if packed is not None:
            work[...] = jnp.where(lane == row + k_all, 1.0, 0.0).astype(F32)
            for c in range(2):
                work[pl.ds(c * k_quarter, k_quarter), :k_all] = packed[c, :, :k_all]
                work[pl.ds(k_half + c * k_quarter, k_quarter), :k_all] = packed[c, :, k_all:]
        v = work[start:, :]
        for j in range(start, stop, PANEL):
            below = lax.broadcasted_iota(jnp.int32, v.shape, 0)
            col = [jnp.broadcast_to(v[:, j + m : j + m + 1], v.shape) for m in range(PANEL)]
            line = [v[m : m + 1, :] for m in range(PANEL)]
            for m in range(PANEL):
                factor = jnp.where(below > m, col[m], 0.0) * (1.0 / col[m][m : m + 1, :])
                for n in range(m + 1, PANEL):
                    line[n] = line[n] - factor[n : n + 1, :] * line[m]
                    col[n] = col[n] - factor * col[n][m : m + 1, :]
                v = v - factor * line[m]
            done, v = v[:PANEL], v[PANEL:]
            mine = (lane == row + j)[:PANEL]
            diag = jnp.sum(jnp.where(mine, done, 0.0), axis=1, keepdims=True)
            invs[i, j : j + PANEL, :] = (done * lax.rsqrt(diag))[:, k_all:]
        if stop < k_all:
            work[stop:, :] = v

    def apply_a(i, low):
        return exact(invs[i, :k_half, :k_half], low)

    def apply_b(i, low, high):
        return exact(invs[i, k_half:, :k_half], low) + exact(invs[i, k_half:, k_half:], high)

    sketch_copy.wait()
    for h in range(2):
        split(sketch[halves[h], :], h, slice(None))

    for dy in far_first(n_y):
        a_copies[dy].wait()
        tm_multiply(0, (0, 1), dy)
    pl.semaphore_wait(barrier, len(greeted))
    for h in range(2):
        for dy in far_first(n_y):
            tm_send(0, h, dy)

    def turn(i, carry):
        block = pl.ds(pl.multiple_of(i * 2 * LANES, 2 * LANES), 2 * LANES)
        a_turned[:, block] = a[block, :].T
        return carry

    lax.fori_loop(0, rows // (2 * LANES), turn, 0)
    for h in range(2):
        tm_gather(0, h, tm_sum(0, h))
    tm_take(0, 0, flats.at[0])

    z_product(0, 0)
    tm_take(0, 1, flats.at[0])
    gram_z_send(0, flats.at[0])
    z_both(0, 0, 0)
    z_product(0, 1, (0, lambda: gram_z_pair(0)))
    z_both(0, 1, 0)
    z_gather(0, 0, z_sum(0, 0))
    gram_z_middle(0)
    z_gather(0, 1, z_sum(0, 1))
    invert(0, gram_end(0))
    z_forward(0, 0)
    z_take(0, 0, flats.at[1])

    tm_product(1, 0, (2, lambda: z_forward(0, 1)))
    z_take(0, 1, flats.at[1])
    tm_product(1, 1)
    tm_low[...] = tm_sum(1, 0)
    tm_gather(1, 0, apply_a(0, tm_low[...]))
    back_flat[...] = exact(invs[0], flats[1])
    gram_tm_send(1, back_flat)
    first_out[...] = (rows_total**0.5) * exact(invs[0], flats[0])
    tm_gather(1, 1, apply_b(0, tm_low[...], tm_sum(1, 1)))
    tm_take(1, 0, flats.at[2])

    z_product(1, 0, (1, lambda: gram_tm_middle(1)))
    packed = gram_end(1)
    z_both(1, 0, 0)
    invert(1, packed, 0, k_half)
    tm_take(1, 1, flats.at[2])
    z_product(1, 1)
    z_both(1, 1, 0)
    z_low[...] = z_sum(1, 0)
    z_gather(1, 0, apply_a(1, z_low[...]))
    invert(1, None, k_half)
    basis_flat[...] = exact(invs[1], flats[2])
    gram_z_send(2, basis_flat)
    gram_z_pair(2)
    z_gather(1, 1, apply_b(1, z_low[...], z_sum(1, 1)))
    back_out[...] = (cols_total**0.5) * exact(invs[1], back_flat[...])
    z_forward(1, 0)
    gram_z_middle(2)
    invert(2, gram_end(2))
    z_forward(1, 1)
    basis_out[...] = (rows_total**0.5) * exact(invs[2], basis_flat[...])
    z_take(1, 0, flats.at[3], again=False)
    proj_out[:k_half, :] = exact(invs[2, :k_half, :k_half], flats[3, :k_half, :])
    z_take(1, 1, flats.at[3], again=False)
    proj_out[k_half:, :] = exact(invs[2, k_half:, :], flats[3])

    for stage in range(2):
        for h in range(2):
            settle(tm_in.at[stage, pl.ds(0, n_t - 1), halves[h], :], tm_rs_s.at[stage, h])
            settle(z_in.at[stage, pl.ds(0, n_z - 1), halves[h], :], z_rs_s.at[stage, h])
            settle(tm_full.at[stage, pl.ds(0, n_t - 1), halves[h], :], tm_ag_s.at[stage, h])
            settle(z_full.at[stage, core, pl.ds(0, n_z - 1), halves[h], :], z_ag_s.at[stage, h])
            settle(z_full.at[stage, core, :, halves[h], :], fw_s.at[stage, h])
            for dg in range(n_g):
                settle(sib_in.at[stage, pl.ds(0, 2), halves[h], :], sib_s.at[stage, h, dg])
        settle(g_z.at[stage, pl.ds(0, n_z - 1)], g_s.at[2 * stage])
        settle(g_pair.at[stage], gp_s.at[stage])
    settle(g_tm.at[pl.ds(0, n_t - 1)], g_s.at[1])
    for i in range(3):
        settle(g_sum.at[i, core], gs_s.at[i])


def finish(*refs):
    sems = refs[-1]
    copies = [pltpu.make_async_copy(refs[i], refs[4 + i], sems.at[i]) for i in range(4)]
    for copy in copies:
        copy.start()
    for copy in copies:
        copy.wait()


def solution(mesh):
    n_s, n_t = mesh.shape["series"], mesh.shape["tm"]
    n_z, n_g = n_s // 2, n_s // 4

    def local(traffic, sketch):
        rows, cols = traffic.shape
        k = sketch.shape[1]
        vmem, hbm, anywhere = (pl.BlockSpec(memory_space=m) for m in (pltpu.VMEM, pltpu.HBM, pl.ANY))
        sem = pltpu.SemaphoreType.DMA
        chunk = (k, LANES)
        gram = (k // 4, 2 * k)
        by_rows, by_cols = jax.ShapeDtypeStruct((k, rows), F32), jax.ShapeDtypeStruct((k, cols), F32)
        outs = pl.pallas_call(
            functools.partial(kernel, n_s, n_t),
            out_shape=(by_rows, by_cols, by_rows, by_cols),
            in_specs=[hbm, hbm],
            out_specs=(vmem,) * 4,
            scratch_shapes=[
                pltpu.VMEM((rows, cols), BF16),
                pltpu.VMEM((cols, rows), BF16),
                pltpu.VMEM((k, cols), F32),
                pltpu.VMEM((3 * k, cols), BF16),
                pltpu.VMEM((2, n_t, *chunk), F32),
                pltpu.VMEM((2, n_t, *chunk), F32),
                pltpu.VMEM((2, n_t, *chunk), F32),
                pltpu.VMEM((2, 2, n_z, *chunk), F32),
                pltpu.VMEM((2, n_z, *chunk), F32),
                pltpu.VMEM((2, n_z, *chunk), F32),
                pltpu.VMEM((2, n_z, *chunk), F32),
                pltpu.VMEM((2, 2, n_z, *chunk), F32),
                pltpu.VMEM((4, k, cols), F32),
                pltpu.VMEM((k, cols), F32),
                pltpu.VMEM((k, rows), F32),
                pltpu.VMEM((k // 2, LANES), F32),
                pltpu.VMEM((k // 2, LANES), F32),
                pltpu.VMEM((3, k, k), F32),
                pltpu.VMEM((k, 2 * k), F32),
                pltpu.VMEM((3, 2, *gram), F32),
                pltpu.VMEM((2, *gram), F32),
                pltpu.VMEM((n_t, *gram), F32),
                pltpu.VMEM((2, n_z, *gram), F32),
                pltpu.VMEM((3, 2, *gram), F32),
                sem((math.isqrt(n_t),)), sem,
                sem((2, 2)), sem((2, 2)), sem((2, 2)), sem((2, 2)),
                sem((2, 2, n_g)), sem((2, 2, n_g)),
                sem((2, 2)), sem((2, 2)), sem((2, 2)), sem((2, 2)), sem((2, 2)), sem((2, 2)),
                sem((2,)), sem((2,)), sem((3,)), sem((3,)), sem((3,)), sem((3,)),
            ],
            compiler_params=pltpu.CompilerParams(
                collective_id=0, has_side_effects=True, vmem_limit_bytes=48 * 2**20
            ),
            name="range_finder",
        )(traffic, pltpu.with_memory_space_constraint(sketch.T, pltpu.HBM))
        first, back, basis, proj = pl.pallas_call(
            finish,
            out_shape=(by_rows, by_cols, by_rows, by_cols),
            in_specs=[anywhere] * 4,
            out_specs=(anywhere,) * 4,
            scratch_shapes=[sem((4,))],
            compiler_params=pltpu.CompilerParams(vmem_limit_bytes=8 * 2**20),
            name="finish",
        )(*outs)
        return first.T, back.T, basis.T, proj

    in_specs = (P("series", "tm"), P("tm", None))
    out_specs = (P("series", None), P("tm", None), P("series", None), P(None, "tm"))
    return jax.shard_map(local, mesh=mesh, in_specs=in_specs, out_specs=out_specs, check_vma=False)
```
